512 devices in a mesh: head: 8 (over x_lo, y), ctx: 64 (over z, x_hi, core).
Axes of the slice: x: 4 (x_hi: 2, x_lo: 2; x = x_hi * 2 + x_lo), y: 4, z: 16, core: 2. Of those that a mesh axis runs over, the one named last changes fastest.
Arguments:
- queries: bfloat16 [65536, 1024], P(('ctx', 'head')), may hold values from -10.5 to 10.5
- key_rows: bfloat16 [65536, 1024], P(('ctx', 'head')), may hold values from -10.5 to 10.5
- value_rows: bfloat16 [65536, 1024], P(('ctx', 'head')), may hold values from -40 to 40
- cotangent: bfloat16 [65536, 1024], P(('ctx', 'head')), may hold values from -20 to 20
- block_list: int32 [512, 8], replicated, may hold values from 0 to 511, as said below
Outputs:
- attended: bfloat16 [65536, 1024], P(('ctx', 'head'))
- query_grad: bfloat16 [65536, 1024], P(('ctx', 'head'))
- key_grad: bfloat16 [65536, 1024], P(('ctx', 'head'))
- value_grad: bfloat16 [65536, 1024], P(('ctx', 'head'))
The draws below stay inside these ranges and needn't reach their ends.
Inputs may be any that keep to these rules, and one draw needn't show every extreme that they name: `block_list`: entry 0 of row a is a itself; the other entries that differ from a are distinct. All rows of one ctx index have the same number of entries that differ from a, at least one; some ctx index has none equal to a past entry 0. Every listed block b satisfies |b // 8 - a // 8| <= 2, and every row lists a block whose distance is exactly 2.
All inputs are finite; a program needn't handle non-finite values.
Results may differ from the reference program's by a relative error of at most 0.038.
Values may be sent and summed in bfloat16 or wider, within the bound.
No kernel may reach another device: no remote copies, remote signals or barrier semaphores. Data moves between devices by JAX's collectives and lax.ppermute only.
A program may use at most 64 MiB of HBM per device.

```python
import jax
import jax.numpy as jnp
from jax import lax

HEADS = 16
HEAD_SIZE = 64
D = 1024
BLOCK = 128
REACH = 2
QBLOCKS = 8
SLOTS = 8
NBLOCKS = 512
SEQ = 65536


def mask_parts(key):
    devices = NBLOCKS // QBLOCKS
    folded = jax.random.fold_in(key, 101)
    subkeys = jax.random.split(folded, 6)
    blocks = jnp.arange(NBLOCKS, dtype=jnp.int32)
    device = blocks // QBLOCKS
    toward = jnp.where(jax.random.randint(subkeys[0], (NBLOCKS,), 0, 2) == 0, -1, 1)
    target = device + toward * REACH
    target = jnp.where((target < 0) | (target >= devices), device - toward * REACH, target)
    distant = target * QBLOCKS + jax.random.randint(subkeys[1], (NBLOCKS,), 0, QBLOCKS)
    listed = [blocks[:, None], distant[:, None]]
    if SLOTS > 2:
        window = (2 * REACH + 1) * QBLOCKS
        offsets = jnp.arange(window, dtype=jnp.int32)
        candidate = (device[:, None] - REACH) * QBLOCKS + offsets[None, :]
        usable = (candidate >= 0) & (candidate < NBLOCKS) & (candidate != blocks[:, None]) & (candidate != distant[:, None])
        jitter = jax.random.randint(subkeys[2], (NBLOCKS, window), 0, 1 << 20)
        ranking = jnp.where(usable, jitter * window + offsets[None, :], -1 - offsets[None, :])
        chosen = lax.top_k(ranking, SLOTS - 2)[1]
        listed.append(jnp.take_along_axis(candidate, chosen, axis=1))
    entries = jnp.concatenate(listed, axis=1)
    crowded = jax.random.randint(subkeys[3], (devices,), 0, 4) == 0
    modest = 2 + jax.random.randint(subkeys[4], (devices,), 0, max(1, SLOTS // 2 - 1))
    forced = jax.random.randint(subkeys[5], (), 0, devices)
    levels = jnp.where(crowded | (jnp.arange(devices, dtype=jnp.int32) == forced), SLOTS, jnp.minimum(modest, SLOTS))
    counts = levels[device].astype(jnp.int32)
    slot_number = jnp.arange(SLOTS, dtype=jnp.int32)
    entries = jnp.where(slot_number[None, :] < counts[:, None], entries, blocks[:, None])
    return entries.astype(jnp.int32)


def draw_block_list(key, part):
    return mask_parts(key)


def draw_queries(key, part):
    key = jax.random.fold_in(key, 5)
    return jnp.clip(jax.random.normal(key, (SEQ, D)), -6.0, 6.0).astype(jnp.bfloat16)


def draw_key_rows(key, part):
    key = jax.random.fold_in(key, 7)
    return jnp.clip(jax.random.normal(key, (SEQ, D)), -6.0, 6.0).astype(jnp.bfloat16)


def block_scale(own_key, shape, pieces, smallest, largest):
    level = 1.0
    for dim, parts in pieces:
        heights = jax.random.uniform(jax.random.fold_in(jax.random.fold_in(own_key, 6), dim), (parts,), jnp.float32, smallest / len(pieces), largest / len(pieces))
        level = level * jnp.repeat(jnp.exp(heights), shape[dim] // parts).reshape((-1,) + (1,) * (len(shape) - 1 - dim))
    return level


def normal_values(stream_key, shape, spread, limit, pieces=(), held_as=jnp.bfloat16):
    gain = block_scale(stream_key, shape, pieces, -0.22, 0.18) if pieces else 1.0
    values = jax.random.normal(stream_key, shape, jnp.float32) * spread * gain
    return jnp.minimum(jnp.maximum(values, -limit), limit).astype(held_as)


def setup_inputs(seed: int = 0) -> dict:
    key_of = jax.random.split(jax.random.key(seed), 6)
    return {
        "queries": draw_queries(jax.random.fold_in(key_of[5], 71), 0),
        "key_rows": draw_key_rows(jax.random.fold_in(key_of[5], 71), 0),
        "value_rows": normal_values(key_of[2], (SEQ, D), 8.0, 40.0, ((0, 512),)),
        "cotangent": normal_values(key_of[3], (SEQ, D), 4.0, 20.0, ((0, 512),)),
        "block_list": draw_block_list(jax.random.fold_in(key_of[5], 71), 0),
    }


def reference(queries, key_rows, value_rows, cotangent, block_list):
    scaling = HEAD_SIZE ** -0.5

    def as_blocks(array):
        return array.reshape(NBLOCKS, BLOCK, HEADS, HEAD_SIZE)

    query_blocks = as_blocks(queries)
    key_blocks = as_blocks(key_rows)
    value_blocks = as_blocks(value_rows)
    grad_blocks = as_blocks(cotangent)
    slot_number = jnp.arange(SLOTS, dtype=jnp.int32)

    def scored(index):
        listed = block_list[index]
        alive = (slot_number == 0) | (listed != index)
        query_block = query_blocks[index].astype(jnp.float32)
        gathered = key_blocks[listed].astype(jnp.float32)
        scores = jnp.einsum("qhd,jkhd->hqjk", query_block, gathered) * scaling
        scores = jnp.where(alive[None, None, :, None], scores, -jnp.inf)
        return listed, scores

    def forward(index):
        listed, scores = scored(index)
        row_max = jnp.max(scores, axis=(2, 3))
        weights = jnp.exp(scores - row_max[:, :, None, None])
        totals = jnp.sum(weights, axis=(2, 3))
        probs = lax.optimization_barrier(weights.astype(jnp.bfloat16)).astype(jnp.float32)
        values = value_blocks[listed].astype(jnp.float32)
        mixed = jnp.einsum("hqjk,jkhd->qhd", probs, values) / jnp.transpose(totals)[:, :, None]
        return mixed.astype(jnp.bfloat16), row_max + jnp.log(totals)

    indices = jnp.arange(NBLOCKS, dtype=jnp.int32)
    attended_blocks, log_totals = lax.map(forward, indices)

    def backward(carry, index):
        key_accum, value_accum = carry
        listed, scores = scored(index)
        recomputed = jnp.exp(scores - log_totals[index][:, :, None, None])
        recomputed_b = lax.optimization_barrier(recomputed.astype(jnp.bfloat16)).astype(jnp.float32)
        grad_block = grad_blocks[index].astype(jnp.float32)
        out_block = attended_blocks[index].astype(jnp.float32)
        delta = jnp.transpose(jnp.sum(grad_block * out_block, axis=2))
        values = value_blocks[listed].astype(jnp.float32)
        gathered = key_blocks[listed].astype(jnp.float32)
        value_part = jnp.einsum("hqjk,qhd->jkhd", recomputed_b, grad_block)
        dprob = jnp.einsum("qhd,jkhd->hqjk", grad_block, values)
        dscore = recomputed * (dprob - delta[:, :, None, None])
        dscore_b = lax.optimization_barrier(dscore.astype(jnp.bfloat16)).astype(jnp.float32)
        query_part = (jnp.einsum("hqjk,jkhd->qhd", dscore_b, gathered) * scaling).astype(jnp.bfloat16)
        key_part = jnp.einsum("hqjk,qhd->jkhd", dscore_b, query_blocks[index].astype(jnp.float32)) * scaling
        key_accum = key_accum.at[listed].add(key_part)
        value_accum = value_accum.at[listed].add(value_part)
        return (key_accum, value_accum), query_part

    zeros = jnp.zeros((NBLOCKS, BLOCK, HEADS, HEAD_SIZE), jnp.float32)
    (key_accum, value_accum), query_parts = lax.scan(backward, (zeros, zeros), indices)
    return (attended_blocks.reshape(SEQ, D), query_parts.reshape(SEQ, D), key_accum.astype(jnp.bfloat16).reshape(SEQ, D), value_accum.astype(jnp.bfloat16).reshape(SEQ, D))
```

```python
import jax
import jax.numpy as jnp
import numpy as np
from jax import lax
from jax.experimental import pallas as pl
from jax.experimental.pallas import tpu as pltpu
from jax.sharding import Mesh, PartitionSpec as P

HEADS = 16
HEAD_SIZE = 64
BLOCK = 128
WIDTH = 2 * HEAD_SIZE
SCALING = HEAD_SIZE ** (-0.5)
PLANE = 32
HALF = PLANE // 2
SLOTS = 8
AXES = ("x_hi", "core", "x_lo", "y")
VMEM_LIMIT = 40 * 1024 * 1024


def lane_pair(left, right, odd):
    start = HEAD_SIZE if odd else 0
    return jnp.concatenate(
        [left[:, start : start + HEAD_SIZE], right[:, start : start + HEAD_SIZE]], axis=1
    )


def slot_of(head, core):
    return (head // 8) * 16 + core * 8 + head % 8


def pack_kernel(place, q_ref, k_ref, v_ref, g_ref, out_ref):
    x_hi = place[1]
    for pair in range(HEADS // 2):
        columns = slice(pair * WIDTH, (pair + 1) * WIDTH)
        q, k, v, g = q_ref[:, columns], k_ref[:, columns], v_ref[:, columns], g_ref[:, columns]
        for odd in range(2):
            head = 2 * pair + odd
            out_ref[slot_of(head, x_hi)] = lane_pair(k, v, odd)
            out_ref[slot_of(head, 1 - x_hi)] = lane_pair(q, g, odd)


def unpack_kernel(place, in_ref, o_ref, dq_ref, dk_ref, dv_ref):
    x_hi = place[1]
    for pair in range(HEADS // 2):
        columns = slice(pair * WIDTH, (pair + 1) * WIDTH)
        even, odd = 2 * pair, 2 * pair + 1
        kv0, kv1 = in_ref[slot_of(even, x_hi)], in_ref[slot_of(odd, x_hi)]
        qo0, qo1 = in_ref[slot_of(even, 1 - x_hi)], in_ref[slot_of(odd, 1 - x_hi)]
        dk_ref[:, columns] = lane_pair(kv0, kv1, 0)
        dv_ref[:, columns] = lane_pair(kv0, kv1, 1)
        dq_ref[:, columns] = lane_pair(qo0, qo1, 0)
        o_ref[:, columns] = lane_pair(qo0, qo1, 1)


def attention_kernel(
    place, index, alive, qg_ref, own_ref, mate_ref, halo_ref,
    qo_ref, own_out, mate_out, halo_out, window, accum, sems,
):
    core = place[0]
    own_at = 2 * core
    halo_at = 2 - own_at
    copies = [
        pltpu.make_async_copy(own_ref, window.at[pl.ds(own_at * HALF, HALF)], sems.at[0]),
        pltpu.make_async_copy(mate_ref, window.at[pl.ds(HALF, HALF)], sems.at[1]),
        pltpu.make_async_copy(halo_ref, window.at[pl.ds(halo_at * HALF, HALF)], sems.at[2]),
    ]
    for copy in copies:
        copy.start()
    accum[...] = jnp.zeros_like(accum)
    for copy in copies:
        copy.wait()
    lane = lax.broadcasted_iota(jnp.int32, (BLOCK, WIDTH), 1)
    left = lane < HEAD_SIZE

    def step(i, carry):
        qg = qg_ref[i]
        zero = jnp.zeros_like(qg)
        rows = jnp.concatenate(
            [jnp.where(left, qg * jnp.bfloat16(SCALING), zero), jnp.where(left, zero, qg)], axis=0
        )
        listed = [index[i, s] for s in range(SLOTS)]
        kv = jnp.concatenate([window[b] for b in listed], axis=0)
        both = lax.dot_general(
            rows, kv, (((1,), (1,)), ((), ())), preferred_element_type=jnp.float32
        )
        scores = jnp.concatenate(
            [
                jnp.where(
                    alive[i, s] > 0, both[:BLOCK, s * BLOCK : (s + 1) * BLOCK], -jnp.inf
                )
                for s in range(SLOTS)
            ],
            axis=1,
        )
        dprob = both[BLOCK:]
        row_max = jnp.max(scores, axis=1, keepdims=True)
        weights = jnp.exp(scores - row_max)
        totals = jnp.sum(weights, axis=1, keepdims=True)
        probs = weights * (1.0 / totals)
        terms = probs * dprob
        delta = jnp.sum(terms, axis=1, keepdims=True)
        dscore = terms - probs * delta
        stacked = jnp.concatenate(
            [dscore.astype(jnp.bfloat16), probs.astype(jnp.bfloat16)], axis=0
        )
        mixed = jnp.dot(stacked, kv, preferred_element_type=jnp.float32)
        qo_ref[i] = jnp.where(left, mixed[:BLOCK] * SCALING, mixed[BLOCK:]).astype(jnp.bfloat16)
        grads = lax.dot_general(
            stacked, rows, (((0,), (0,)), ((), ())), preferred_element_type=jnp.float32
        )
        for s in range(SLOTS):
            accum[listed[s]] += grads[s * BLOCK : (s + 1) * BLOCK]
        return carry

    lax.fori_loop(0, HALF, step, 0)
    own_out[...] = accum[pl.ds(own_at * HALF, HALF)]
    mate_out[...] = accum[HALF : 2 * HALF].astype(jnp.bfloat16)
    halo_out[...] = accum[pl.ds(halo_at * HALF, HALF)].astype(jnp.bfloat16)


def sum_kernel(place, qo_ref, own_ref, mate_ref, halo_ref, out_ref):
    core = place[0]
    total = own_ref[...] + mate_ref[...].astype(jnp.float32) + halo_ref[...].astype(jnp.float32)
    out_ref[pl.ds(core * HALF, HALF)] = total.astype(jnp.bfloat16)
    out_ref[pl.ds((1 - core) * HALF, HALF)] = qo_ref[...]


SMEM = pl.BlockSpec(memory_space=pltpu.SMEM)
VMEM = pl.BlockSpec(memory_space=pltpu.VMEM)
ANY = pl.BlockSpec(memory_space=pl.ANY)
PARAMS = pltpu.CompilerParams(vmem_limit_bytes=VMEM_LIMIT)


def moved(value, axes, target):
    sizes = [lax.axis_size(a) for a in axes]
    pairs = []
    for source in range(int(np.prod(sizes))):
        spot = [int(t) for t in np.unravel_index(source, sizes)]
        pairs.append((source, int(np.ravel_multi_index(target(*spot), sizes))))
    return lax.ppermute(value, axes, pairs)


def to_mate(value):
    return moved(value, ("core",), lambda c: (1 - c,))


def per_device(queries, key_rows, value_rows, cotangent, block_list):
    depth = lax.axis_size("z")
    core, x_hi, z = lax.axis_index("core"), lax.axis_index("x_hi"), lax.axis_index("z")
    place = jnp.stack([core, x_hi]).astype(jnp.int32)
    packed = pl.pallas_call(
        pack_kernel,
        out_shape=jax.ShapeDtypeStruct((PLANE, BLOCK, WIDTH), jnp.bfloat16),
        in_specs=[SMEM] + [VMEM] * 4,
        out_specs=VMEM,
        compiler_params=PARAMS,
        name="pack",
    )(place, queries, key_rows, value_rows, cotangent)
    received = lax.all_to_all(packed, AXES, 0, 0, tiled=True)
    key_value = lax.dynamic_slice_in_dim(received, core * HALF, HALF, 0)
    query_grad_rows = lax.dynamic_slice_in_dim(received, (1 - core) * HALF, HALF, 0)
    mate = to_mate(key_value)
    halo = moved(
        key_value, ("z", "core"), lambda z, c: ((z + (1 if c else depth - 1)) % depth, c)
    )
    first_query = z * PLANE + (1 - core) * HALF
    first_key = z * PLANE - core * HALF
    listed = lax.dynamic_slice_in_dim(block_list, first_query, HALF, 0)
    own_blocks = first_query + jnp.arange(HALF, dtype=jnp.int32)
    alive = (jnp.arange(SLOTS)[None, :] == 0) | (listed != own_blocks[:, None])
    index = listed - first_key
    half = (HALF, BLOCK, WIDTH)
    query_out, own_part, mate_part, halo_part = pl.pallas_call(
        attention_kernel,
        out_shape=[
            jax.ShapeDtypeStruct(half, jnp.bfloat16),
            jax.ShapeDtypeStruct(half, jnp.float32),
            jax.ShapeDtypeStruct(half, jnp.bfloat16),
            jax.ShapeDtypeStruct(half, jnp.bfloat16),
        ],
        in_specs=[SMEM] * 3 + [VMEM] + [ANY] * 3,
        out_specs=[VMEM] * 4,
        scratch_shapes=[
            pltpu.VMEM((3 * HALF, BLOCK, WIDTH), jnp.bfloat16),
            pltpu.VMEM((3 * HALF, BLOCK, WIDTH), jnp.float32),
            pltpu.SemaphoreType.DMA((3,)),
        ],
        compiler_params=PARAMS,
        name="attention",
    )(place, index, alive.astype(jnp.int32), query_grad_rows, key_value, mate, halo)
    mate_sum = to_mate(mate_part)
    halo_sum = moved(
        halo_part, ("z", "core"), lambda z, c: ((z + (depth - 1 if c else 1)) % depth, c)
    )
    outgoing = pl.pallas_call(
        sum_kernel,
        out_shape=jax.ShapeDtypeStruct((PLANE, BLOCK, WIDTH), jnp.bfloat16),
        in_specs=[SMEM] + [VMEM] * 4,
        out_specs=VMEM,
        compiler_params=PARAMS,
        name="total",
    )(place, query_out, own_part, mate_sum, halo_sum)
    returned = lax.all_to_all(outgoing, AXES, 0, 0, tiled=True)
    rows = jax.ShapeDtypeStruct(queries.shape, jnp.bfloat16)
    return pl.pallas_call(
        unpack_kernel,
        out_shape=[rows] * 4,
        in_specs=[SMEM, VMEM],
        out_specs=[VMEM] * 4,
        compiler_params=PARAMS,
        name="unpack",
    )(place, returned)


def solution(mesh):
    fine = Mesh(mesh.devices.reshape(2, 4, 16, 2, 2), ("x_lo", "y", "z", "x_hi", "core"))
    rows = P(("z", "x_hi", "core", "x_lo", "y"), None)
    return jax.shard_map(
        per_device,
        mesh=fine,
        in_specs=(rows,) * 4 + (P(),),
        out_specs=(rows,) * 4,
        check_vma=False,
    )
```

```python
import jax
import jax.numpy as jnp
import numpy as np
from jax import lax
from jax.experimental import pallas as pl
from jax.experimental.pallas import tpu as pltpu
from jax.sharding import Mesh, PartitionSpec as P

HEADS = 16
HEAD_SIZE = 64
BLOCK = 128
WIDTH = 2 * HEAD_SIZE
SCALING = HEAD_SIZE ** (-0.5)
PLANE = 32
HALF = PLANE // 2
SLOTS = 8
AXES = ("x_hi", "core", "x_lo", "y")
VMEM_LIMIT = 40 * 1024 * 1024
KEYS = SLOTS * BLOCK
CHUNK = 16
PART = 256
PARTS = HEADS * HEAD_SIZE // PART


def lane_pair(left, right, odd):
    start = HEAD_SIZE if odd else 0
    return jnp.concatenate(
        [left[:, start : start + HEAD_SIZE], right[:, start : start + HEAD_SIZE]], axis=1
    )


def slot_of(head, core):
    return (head // 8) * 16 + core * 8 + head % 8


def pack_kernel(place, q_hbm, k_hbm, v_hbm, g_hbm, out_ref, q_ref, k_ref, v_ref, g_ref, sems):
    x_hi = place[1]
    parts = [slice(p * PART, (p + 1) * PART) for p in range(PARTS)]
    copies = [
        [
            pltpu.make_async_copy(source.at[:, part], target.at[:, part], sems.at[p, n])
            for n, (source, target) in enumerate(
                ((k_hbm, k_ref), (v_hbm, v_ref), (q_hbm, q_ref), (g_hbm, g_ref))
            )
        ]
        for p, part in enumerate(parts)
    ]
    for group in copies:
        for copy in group:
            copy.start()
    for pair in range(HEADS // 2):
        if pair * WIDTH % PART == 0:
            for copy in copies[pair * WIDTH // PART]:
                copy.wait()
        columns = slice(pair * WIDTH, (pair + 1) * WIDTH)
        q, k, v, g = q_ref[:, columns], k_ref[:, columns], v_ref[:, columns], g_ref[:, columns]
        for odd in range(2):
            head = 2 * pair + odd
            out_ref[slot_of(head, x_hi)] = lane_pair(k, v, odd)
            out_ref[slot_of(head, 1 - x_hi)] = lane_pair(q, g, odd)


def unpack_kernel(
    place, in_ref, o_hbm, dq_hbm, dk_hbm, dv_hbm, o_ref, dq_ref, dk_ref, dv_ref, sems
):
    x_hi = place[1]
    copies = []
    for pair in range(HEADS // 2):
        columns = slice(pair * WIDTH, (pair + 1) * WIDTH)
        even, odd = 2 * pair, 2 * pair + 1
        kv0, kv1 = in_ref[slot_of(even, x_hi)], in_ref[slot_of(odd, x_hi)]
        qo0, qo1 = in_ref[slot_of(even, 1 - x_hi)], in_ref[slot_of(odd, 1 - x_hi)]
        dk_ref[:, columns] = lane_pair(kv0, kv1, 0)
        dv_ref[:, columns] = lane_pair(kv0, kv1, 1)
        dq_ref[:, columns] = lane_pair(qo0, qo1, 0)
        o_ref[:, columns] = lane_pair(qo0, qo1, 1)
        if (pair + 1) * WIDTH % PART == 0:
            p = pair * WIDTH // PART
            part = slice(p * PART, (p + 1) * PART)
            for n, (source, target) in enumerate(
                ((o_ref, o_hbm), (dq_ref, dq_hbm), (dk_ref, dk_hbm), (dv_ref, dv_hbm))
            ):
                copy = pltpu.make_async_copy(source.at[:, part], target.at[:, part], sems.at[p, n])
                copy.start()
                copies.append(copy)
    for copy in copies:
        copy.wait()


def attention_kernel(
    place, index, alive, qg_ref, own_ref, mate_ref, halo_ref,
    qo_ref, own_out, mate_out, halo_out,
    window, accum, both_even, both_odd, pair_even, pair_odd, sems,
):
    core = place[0]
    own_at = 2 * core
    halo_at = 2 - own_at
    copies = [
        pltpu.make_async_copy(own_ref, window.at[pl.ds(own_at * HALF, HALF)], sems.at[0]),
        pltpu.make_async_copy(mate_ref, window.at[pl.ds(HALF, HALF)], sems.at[1]),
        pltpu.make_async_copy(halo_ref, window.at[pl.ds(halo_at * HALF, HALF)], sems.at[2]),
    ]
    for copy in copies:
        copy.start()
    accum[...] = jnp.zeros_like(accum)
    pair_odd[...] = jnp.zeros_like(pair_odd)
    for copy in copies:
        copy.wait()
    left = lax.broadcasted_iota(jnp.int32, (BLOCK, WIDTH), 1) < HEAD_SIZE

    def listed_rows(i):
        return jnp.concatenate([window[index[i, s]] for s in range(SLOTS)], axis=0)

    def query_rows(i):
        qg = qg_ref[i]
        zero = jnp.zeros_like(qg)
        return jnp.concatenate(
            [jnp.where(left, qg * jnp.bfloat16(SCALING), zero), jnp.where(left, zero, qg)], axis=0
        )

    def products(i, both):
        both[...] = lax.dot_general(
            query_rows(i), listed_rows(i), (((1,), (1,)), ((), ())),
            preferred_element_type=jnp.float32,
        )

    def weigh(i, both, pair):
        live = [alive[i, s] > 0 for s in range(SLOTS)]
        for r in range(0, BLOCK, CHUNK):
            scores = jnp.concatenate(
                [
                    jnp.where(live[s], both[r : r + CHUNK, s * BLOCK : (s + 1) * BLOCK], -jnp.inf)
                    for s in range(SLOTS)
                ],
                axis=1,
            )
            dprob = both[BLOCK + r : BLOCK + r + CHUNK]
            weights = jnp.exp(scores - jnp.max(scores, axis=1, keepdims=True))
            probs = weights * (1.0 / jnp.sum(weights, axis=1, keepdims=True))
            terms = probs * dprob
            dscore = terms - probs * jnp.sum(terms, axis=1, keepdims=True)
            pair[r : r + CHUNK] = dscore.astype(jnp.bfloat16)
            pair[BLOCK + r : BLOCK + r + CHUNK] = probs.astype(jnp.bfloat16)

    def results(i, pair):
        stacked = pair[...]
        mixed = jnp.dot(stacked, listed_rows(i), preferred_element_type=jnp.float32)
        qo_ref[i] = jnp.where(left, mixed[:BLOCK] * SCALING, mixed[BLOCK:]).astype(jnp.bfloat16)
        grads = lax.dot_general(
            stacked, query_rows(i), (((0,), (0,)), ((), ())), preferred_element_type=jnp.float32
        )
        for s in range(SLOTS):
            accum[index[i, s]] += grads[s * BLOCK : (s + 1) * BLOCK]

    products(0, both_even)

    def step(j, carry):
        even, odd = 2 * j, 2 * j + 1
        products(odd, both_odd)
        weigh(even, both_even, pair_even)
        results(jnp.maximum(even - 1, 0), pair_odd)
        products(jnp.minimum(even + 2, HALF - 1), both_even)
        weigh(odd, both_odd, pair_odd)
        results(even, pair_even)
        return carry

    lax.fori_loop(0, HALF // 2, step, 0)
    results(HALF - 1, pair_odd)
    halo_out[...] = accum[pl.ds(halo_at * HALF, HALF)].astype(jnp.bfloat16)
    mate_out[...] = accum[HALF : 2 * HALF].astype(jnp.bfloat16)
    own_out[...] = accum[pl.ds(own_at * HALF, HALF)]


def sum_kernel(place, qo_ref, own_ref, mate_ref, halo_ref, out_ref):
    core = place[0]
    total = own_ref[...] + mate_ref[...].astype(jnp.float32) + halo_ref[...].astype(jnp.float32)
    out_ref[pl.ds(core * HALF, HALF)] = total.astype(jnp.bfloat16)
    out_ref[pl.ds((1 - core) * HALF, HALF)] = qo_ref[...]


SMEM = pl.BlockSpec(memory_space=pltpu.SMEM)
VMEM = pl.BlockSpec(memory_space=pltpu.VMEM)
ANY = pl.BlockSpec(memory_space=pl.ANY)
PARAMS = pltpu.CompilerParams(vmem_limit_bytes=VMEM_LIMIT)
EDGE_PARAMS = pltpu.CompilerParams(vmem_limit_bytes=60 * 1024 * 1024)


def moved(value, axes, target):
    sizes = [lax.axis_size(a) for a in axes]
    pairs = []
    for source in range(int(np.prod(sizes))):
        spot = [int(t) for t in np.unravel_index(source, sizes)]
        pairs.append((source, int(np.ravel_multi_index(target(*spot), sizes))))
    return lax.ppermute(value, axes, pairs)


def to_mate(value):
    return moved(value, ("core",), lambda c: (1 - c,))


def per_device(queries, key_rows, value_rows, cotangent, block_list):
    depth = lax.axis_size("z")
    core, x_hi, z = lax.axis_index("core"), lax.axis_index("x_hi"), lax.axis_index("z")
    place = jnp.stack([core, x_hi]).astype(jnp.int32)
    packed = pl.pallas_call(
        pack_kernel,
        out_shape=jax.ShapeDtypeStruct((PLANE, BLOCK, WIDTH), jnp.bfloat16),
        in_specs=[SMEM] + [ANY] * 4,
        out_specs=VMEM,
        scratch_shapes=[pltpu.VMEM(queries.shape, jnp.bfloat16)] * 4
        + [pltpu.SemaphoreType.DMA((PARTS, 4))],
        compiler_params=EDGE_PARAMS,
        name="pack",
    )(place, queries, key_rows, value_rows, cotangent)
    received = lax.all_to_all(packed, AXES, 0, 0, tiled=True)
    key_value = lax.dynamic_slice_in_dim(received, core * HALF, HALF, 0)
    query_grad_rows = lax.dynamic_slice_in_dim(received, (1 - core) * HALF, HALF, 0)
    mate = to_mate(key_value)
    halo = moved(
        key_value, ("z", "core"), lambda z, c: ((z + (1 if c else depth - 1)) % depth, c)
    )
    first_query = z * PLANE + (1 - core) * HALF
    first_key = z * PLANE - core * HALF
    listed = lax.dynamic_slice_in_dim(block_list, first_query, HALF, 0)
    own_blocks = first_query + jnp.arange(HALF, dtype=jnp.int32)
    alive = (jnp.arange(SLOTS)[None, :] == 0) | (listed != own_blocks[:, None])
    index = listed - first_key
    half = (HALF, BLOCK, WIDTH)
    query_out, own_part, mate_part, halo_part = pl.pallas_call(
        attention_kernel,
        out_shape=[
            jax.ShapeDtypeStruct(half, jnp.bfloat16),
            jax.ShapeDtypeStruct(half, jnp.float32),
            jax.ShapeDtypeStruct(half, jnp.bfloat16),
            jax.ShapeDtypeStruct(half, jnp.bfloat16),
        ],
        in_specs=[SMEM] * 3 + [VMEM] + [ANY] * 3,
        out_specs=[VMEM] * 4,
        scratch_shapes=[
            pltpu.VMEM((3 * HALF, BLOCK, WIDTH), jnp.bfloat16),
            pltpu.VMEM((3 * HALF, BLOCK, WIDTH), jnp.float32),
            pltpu.VMEM((2 * BLOCK, KEYS), jnp.float32),
            pltpu.VMEM((2 * BLOCK, KEYS), jnp.float32),
            pltpu.VMEM((2 * BLOCK, KEYS), jnp.bfloat16),
            pltpu.VMEM((2 * BLOCK, KEYS), jnp.bfloat16),
            pltpu.SemaphoreType.DMA((3,)),
        ],
        compiler_params=PARAMS,
        name="attention",
    )(place, index, alive.astype(jnp.int32), query_grad_rows, key_value, mate, halo)
    mate_sum = to_mate(mate_part)
    halo_sum = moved(
        halo_part, ("z", "core"), lambda z, c: ((z + (depth - 1 if c else 1)) % depth, c)
    )
    outgoing = pl.pallas_call(
        sum_kernel,
        out_shape=jax.ShapeDtypeStruct((PLANE, BLOCK, WIDTH), jnp.bfloat16),
        in_specs=[SMEM] + [VMEM] * 4,
        out_specs=VMEM,
        compiler_params=PARAMS,
        name="total",
    )(place, query_out, own_part, mate_sum, halo_sum)
    returned = lax.all_to_all(outgoing, AXES, 0, 0, tiled=True)
    rows = jax.ShapeDtypeStruct(queries.shape, jnp.bfloat16)
    return pl.pallas_call(
        unpack_kernel,
        out_shape=[rows] * 4,
        in_specs=[SMEM, VMEM],
        out_specs=[ANY] * 4,
        scratch_shapes=[pltpu.VMEM(queries.shape, jnp.bfloat16)] * 4
        + [pltpu.SemaphoreType.DMA((PARTS, 4))],
        compiler_params=PARAMS,
        name="unpack",
    )(place, returned)


def solution(mesh):
    fine = Mesh(mesh.devices.reshape(2, 4, 16, 2, 2), ("x_lo", "y", "z", "x_hi", "core"))
    rows = P(("z", "x_hi", "core", "x_lo", "y"), None)
    return jax.shard_map(
        per_device,
        mesh=fine,
        in_specs=(rows,) * 4 + (P(),),
        out_specs=(rows,) * 4,
        check_vma=False,
    )
```

```python
import jax
import jax.numpy as jnp
import numpy as np
from jax import lax
from jax.experimental import pallas as pl
from jax.experimental.pallas import tpu as pltpu
from jax.sharding import Mesh, PartitionSpec as P

HEADS = 16
HEAD_SIZE = 64
BLOCK = 128
WIDTH = 2 * HEAD_SIZE
SCALING = HEAD_SIZE ** (-0.5)
PLANE = 32
HALF = PLANE // 2
SLOTS = 8
AXES = ("x_hi", "core", "x_lo", "y")
VMEM_LIMIT = 24 * 1024 * 1024
PAIR = 2 * BLOCK
SPARE = 6
LISTED = HALF * SLOTS + 8
LOWEST = -1e30
CHUNK = 16
PART = 256
PARTS = HEADS * HEAD_SIZE // PART


def lane_pair(left, right, odd):
    start = HEAD_SIZE if odd else 0
    return jnp.concatenate(
        [left[:, start : start + HEAD_SIZE], right[:, start : start + HEAD_SIZE]], axis=1
    )


def slot_of(head, core):
    return (head // 8) * 16 + core * 8 + head % 8


def pack_kernel(place, q_hbm, k_hbm, v_hbm, g_hbm, out_ref, q_ref, k_ref, v_ref, g_ref, sems):
    x_hi = place[1]
    parts = [slice(p * PART, (p + 1) * PART) for p in range(PARTS)]
    copies = [
        [
            pltpu.make_async_copy(source.at[:, part], target.at[:, part], sems.at[p, n])
            for n, (source, target) in enumerate(
                ((k_hbm, k_ref), (v_hbm, v_ref), (q_hbm, q_ref), (g_hbm, g_ref))
            )
        ]
        for p, part in enumerate(parts)
    ]
    for group in copies:
        for copy in group:
            copy.start()
    for pair in range(HEADS // 2):
        if pair * WIDTH % PART == 0:
            for copy in copies[pair * WIDTH // PART]:
                copy.wait()
        columns = slice(pair * WIDTH, (pair + 1) * WIDTH)
        q, k, v, g = q_ref[:, columns], k_ref[:, columns], v_ref[:, columns], g_ref[:, columns]
        for odd in range(2):
            head = 2 * pair + odd
            out_ref[slot_of(head, x_hi)] = lane_pair(k, v, odd)
            out_ref[slot_of(head, 1 - x_hi)] = lane_pair(q, g, odd)


def unpack_kernel(
    place, in_ref, o_hbm, dq_hbm, dk_hbm, dv_hbm, o_ref, dq_ref, dk_ref, dv_ref, sems
):
    x_hi = place[1]
    copies = []
    for pair in range(HEADS // 2):
        columns = slice(pair * WIDTH, (pair + 1) * WIDTH)
        even, odd = 2 * pair, 2 * pair + 1
        kv0, kv1 = in_ref[slot_of(even, x_hi)], in_ref[slot_of(odd, x_hi)]
        qo0, qo1 = in_ref[slot_of(even, 1 - x_hi)], in_ref[slot_of(odd, 1 - x_hi)]
        dk_ref[:, columns] = lane_pair(kv0, kv1, 0)
        dv_ref[:, columns] = lane_pair(kv0, kv1, 1)
        dq_ref[:, columns] = lane_pair(qo0, qo1, 0)
        o_ref[:, columns] = lane_pair(qo0, qo1, 1)
        if (pair + 1) * WIDTH % PART == 0:
            p = pair * WIDTH // PART
            part = slice(p * PART, (p + 1) * PART)
            for n, (source, target) in enumerate(
                ((o_ref, o_hbm), (dq_ref, dq_hbm), (dk_ref, dk_hbm), (dv_ref, dv_hbm))
            ):
                copy = pltpu.make_async_copy(source.at[:, part], target.at[:, part], sems.at[p, n])
                copy.start()
                copies.append(copy)
    for copy in copies:
        copy.wait()


def plan_kernel(index, alive, place, local_out, halo_out, count_out):
    plane_at = place[0] * HALF
    halo_at = (1 - place[0]) * PLANE

    def padded(out, spot):
        out[0, spot] = -1
        return spot + spot % 2

    def per_query(i, spots):
        local, halo = spots
        for s in range(SLOTS):
            block, live = index[i, s], alive[i, s]
            here = block - plane_at
            inside = jnp.where((here >= 0) & (here < PLANE), live, 0)
            local_out[0, local] = here
            local_out[1, local] = i
            halo_out[0, halo] = block - halo_at
            halo_out[1, halo] = i
            local = local + inside
            halo = halo + live - inside
        return padded(local_out, local), padded(halo_out, halo)

    local, halo = lax.fori_loop(0, HALF, per_query, (jnp.int32(0), jnp.int32(0)))
    for out, spot in ((local_out, local), (halo_out, halo)):
        for extra in range(SPARE):
            out[0, spot + extra] = -1
            out[1, spot + extra] = HALF - 1
    count_out[0] = local // 2
    count_out[1] = halo // 2


def left_lanes():
    return lax.broadcasted_iota(jnp.int32, (BLOCK, WIDTH), 1) < HEAD_SIZE


def query_rows(queries, tasks, t, left):
    qg = queries[tasks[1, 2 * t]]
    zero = jnp.zeros_like(qg)
    return jnp.concatenate(
        [jnp.where(left, qg * jnp.bfloat16(SCALING), zero), jnp.where(left, zero, qg)], axis=0
    )


def pair_of(tasks, t):
    blocks = [tasks[0, 2 * t], tasks[0, 2 * t + 1]]
    return [jnp.maximum(b, 0) for b in blocks], [b >= 0 for b in blocks]


def listed_rows(window, tasks, t):
    return jnp.concatenate([window[b] for b in pair_of(tasks, t)[0]], axis=0)


def products(queries, window, tasks, t, left, both):
    both[...] = lax.dot_general(
        query_rows(queries, tasks, t, left), listed_rows(window, tasks, t),
        (((1,), (1,)), ((), ())), preferred_element_type=jnp.float32,
    )


def pair_scores(both, live, r):
    return [
        jnp.where(live[s], both[r : r + CHUNK, s * BLOCK : (s + 1) * BLOCK], -jnp.inf)
        for s in range(2)
    ]


def statistics(queries, window, tasks, count, stats, both_even, both_odd):
    left = left_lanes()

    def gather(t, both):
        t_query = tasks[1, 2 * t]
        live = pair_of(tasks, t)[1]
        for r in range(0, BLOCK, CHUNK):
            rows = slice(r, r + CHUNK)
            first, second = pair_scores(both, live, r)
            dprobs = both[BLOCK + r : BLOCK + r + CHUNK]
            old = stats[0, t_query, rows]
            top = jnp.maximum(old, jnp.maximum(first, second))
            kept = jnp.exp(old - top)
            w0, w1 = jnp.exp(first - top), jnp.exp(second - top)
            stats[0, t_query, rows] = top
            stats[1, t_query, rows] = stats[1, t_query, rows] * kept + w0 + w1
            stats[2, t_query, rows] = (
                stats[2, t_query, rows] * kept + w0 * dprobs[:, :BLOCK] + w1 * dprobs[:, BLOCK:]
            )

    products(queries, window, tasks, 0, left, both_even)

    def step(j, carry):
        even, odd = 2 * j, 2 * j + 1
        products(queries, window, tasks, odd, left, both_odd)
        gather(even, both_even)
        products(queries, window, tasks, odd + 1, left, both_even)
        gather(odd, both_odd)
        return carry

    lax.fori_loop(0, (count + 1) // 2, step, 0)


def gradients(
    queries, window, tasks, count, ends, mixed, accum, both_even, both_odd, pair_even, pair_odd
):
    left = left_lanes()
    pair_odd[...] = jnp.zeros_like(pair_odd)

    def weigh(t, both, pair):
        t_query = tasks[1, 2 * t]
        live = pair_of(tasks, t)[1]
        for r in range(0, BLOCK, CHUNK):
            rows = slice(r, r + CHUNK)
            log_totals, delta = ends[0, t_query, rows], ends[1, t_query, rows]
            for s, scores in enumerate(pair_scores(both, live, r)):
                columns = slice(s * BLOCK, (s + 1) * BLOCK)
                probs = jnp.exp(scores - log_totals)
                dscore = probs * (both[BLOCK + r : BLOCK + r + CHUNK, columns] - delta)
                pair[rows, columns] = dscore.astype(jnp.bfloat16)
                pair[BLOCK + r : BLOCK + r + CHUNK, columns] = probs.astype(jnp.bfloat16)

    def results(t, pair):
        t_query = tasks[1, 2 * t]
        stacked = pair[...]
        both = jnp.dot(stacked, listed_rows(window, tasks, t), preferred_element_type=jnp.float32)
        mixed[t_query] += jnp.where(left, both[:BLOCK] * SCALING, both[BLOCK:])
        grads = lax.dot_general(
            stacked, query_rows(queries, tasks, t, left), (((0,), (0,)), ((), ())),
            preferred_element_type=jnp.float32,
        )
        for s, block in enumerate(pair_of(tasks, t)[0]):
            accum[block] += grads[s * BLOCK : (s + 1) * BLOCK]

    products(queries, window, tasks, 0, left, both_even)

    def step(j, carry):
        even, odd = 2 * j, 2 * j + 1
        products(queries, window, tasks, odd, left, both_odd)
        weigh(even, both_even, pair_even)
        results(jnp.maximum(even - 1, 0), pair_odd)
        products(queries, window, tasks, odd + 1, left, both_even)
        weigh(odd, both_odd, pair_odd)
        results(even, pair_even)
        return carry

    steps = (count + 1) // 2
    lax.fori_loop(0, steps, step, 0)
    results(jnp.maximum(2 * steps - 1, 0), pair_odd)


def local_statistics_kernel(
    place, tasks, counts, queries, own_ref, mate_ref, stats, plane, both_even, both_odd, sems
):
    core = place[0]
    copies = [
        pltpu.make_async_copy(own_ref, plane.at[pl.ds(core * HALF, HALF)], sems.at[0]),
        pltpu.make_async_copy(mate_ref, plane.at[pl.ds((1 - core) * HALF, HALF)], sems.at[1]),
    ]
    for copy in copies:
        copy.start()
    stats[0] = jnp.full(stats.shape[1:], LOWEST, jnp.float32)
    stats[1] = jnp.zeros(stats.shape[1:], jnp.float32)
    stats[2] = jnp.zeros(stats.shape[1:], jnp.float32)
    for copy in copies:
        copy.wait()
    statistics(queries, plane, tasks, counts[0], stats, both_even, both_odd)


def halo_kernel(
    tasks, counts, queries, halo_ref, stats_in, ends, mixed, halo_out,
    stats, accum, both_even, both_odd, pair_even, pair_odd, sem,
):
    copy = pltpu.make_async_copy(stats_in, stats, sem)
    copy.start()
    accum[...] = jnp.zeros_like(accum)
    mixed[...] = jnp.zeros_like(mixed)
    copy.wait()
    statistics(queries, halo_ref, tasks, counts[1], stats, both_even, both_odd)

    def finish(i, carry):
        lane_max = stats[0, i]
        row_max = jnp.max(lane_max, axis=1, keepdims=True)
        kept = jnp.exp(lane_max - row_max)
        totals = jnp.sum(stats[1, i] * kept, axis=1, keepdims=True)
        delta = jnp.sum(stats[2, i] * kept, axis=1, keepdims=True) / totals
        ends[0, i] = jnp.broadcast_to(row_max + jnp.log(totals), (BLOCK, WIDTH))
        ends[1, i] = jnp.broadcast_to(delta, (BLOCK, WIDTH))
        return carry

    lax.fori_loop(0, HALF, finish, 0)
    gradients(
        queries, halo_ref, tasks, counts[1], ends, mixed, accum,
        both_even, both_odd, pair_even, pair_odd,
    )
    halo_out[...] = accum[...].astype(jnp.bfloat16)


def local_gradients_kernel(
    place, tasks, counts, queries, plane, ends, mixed_in, qo_ref, own_out, mate_out,
    mixed, accum, both_even, both_odd, pair_even, pair_odd, sem,
):
    core = place[0]
    copy = pltpu.make_async_copy(mixed_in, mixed, sem)
    copy.start()
    accum[...] = jnp.zeros_like(accum)
    copy.wait()
    gradients(
        queries, plane, tasks, counts[0], ends, mixed, accum,
        both_even, both_odd, pair_even, pair_odd,
    )
    qo_ref[...] = mixed[...].astype(jnp.bfloat16)
    mate_out[...] = accum[pl.ds((1 - core) * HALF, HALF)].astype(jnp.bfloat16)
    own_out[...] = accum[pl.ds(core * HALF, HALF)]


def halo_sum_kernel(own_ref, halo_ref, out_ref):
    out_ref[...] = own_ref[...] + halo_ref[...].astype(jnp.float32)


def sum_kernel(place, qo_ref, own_ref, mate_ref, out_ref):
    core = place[0]
    total = own_ref[...] + mate_ref[...].astype(jnp.float32)
    out_ref[pl.ds(core * HALF, HALF)] = total.astype(jnp.bfloat16)
    out_ref[pl.ds((1 - core) * HALF, HALF)] = qo_ref[...]


SMEM = pl.BlockSpec(memory_space=pltpu.SMEM)
VMEM = pl.BlockSpec(memory_space=pltpu.VMEM)
ANY = pl.BlockSpec(memory_space=pl.ANY)
PARAMS = pltpu.CompilerParams(vmem_limit_bytes=VMEM_LIMIT)
EDGE_PARAMS = pltpu.CompilerParams(vmem_limit_bytes=60 * 1024 * 1024)


def moved(value, axes, target):
    sizes = [lax.axis_size(a) for a in axes]
    pairs = []
    for source in range(int(np.prod(sizes))):
        spot = [int(t) for t in np.unravel_index(source, sizes)]
        pairs.append((source, int(np.ravel_multi_index(target(*spot), sizes))))
    return lax.ppermute(value, axes, pairs)


def to_mate(value):
    return moved(value, ("core",), lambda c: (1 - c,))


def cost(pairs):
    flops = pairs * 2 * PAIR * PAIR * WIDTH
    return pl.CostEstimate(flops=flops, bytes_accessed=1 << 20, transcendentals=pairs * BLOCK * PAIR)


HALF_BF16 = jax.ShapeDtypeStruct((HALF, BLOCK, WIDTH), jnp.bfloat16)
HALF_F32 = jax.ShapeDtypeStruct((HALF, BLOCK, WIDTH), jnp.float32)
TASKS = jax.ShapeDtypeStruct((2, LISTED), jnp.int32)
BOTHS = [pltpu.VMEM((PAIR, PAIR), jnp.float32)] * 2
PAIRS = [pltpu.VMEM((PAIR, PAIR), jnp.bfloat16)] * 2


def attention_in(place, index, alive, queries, own, mate):
    local_tasks, halo_tasks, counts = pl.pallas_call(
        plan_kernel,
        out_shape=[TASKS, TASKS, jax.ShapeDtypeStruct((2,), jnp.int32)],
        in_specs=[SMEM] * 3,
        out_specs=[SMEM] * 3,
        name="plan",
    )(index, alive, place)
    stats, plane = pl.pallas_call(
        local_statistics_kernel,
        out_shape=[
            jax.ShapeDtypeStruct((3, HALF, BLOCK, WIDTH), jnp.float32),
            jax.ShapeDtypeStruct((PLANE, BLOCK, WIDTH), jnp.bfloat16),
        ],
        in_specs=[SMEM] * 3 + [VMEM] + [ANY] * 2,
        out_specs=[VMEM] * 2,
        scratch_shapes=BOTHS + [pltpu.SemaphoreType.DMA((2,))],
        compiler_params=PARAMS,
        cost_estimate=cost(64),
        name="local_statistics",
    )(place, local_tasks, counts, queries, own, mate)
    return local_tasks, halo_tasks, counts, stats, plane


def attention_halo(tasks, counts, queries, halo, stats):
    return pl.pallas_call(
        halo_kernel,
        out_shape=[jax.ShapeDtypeStruct((2, HALF, BLOCK, WIDTH), jnp.float32), HALF_F32, HALF_BF16],
        in_specs=[SMEM] * 2 + [VMEM] * 2 + [ANY],
        out_specs=[VMEM] * 3,
        scratch_shapes=[
            pltpu.VMEM((3, HALF, BLOCK, WIDTH), jnp.float32),
            pltpu.VMEM((HALF, BLOCK, WIDTH), jnp.float32),
        ]
        + BOTHS
        + PAIRS
        + [pltpu.SemaphoreType.DMA],
        compiler_params=PARAMS,
        cost_estimate=cost(64),
        name="halo",
    )(tasks, counts, queries, halo, stats)


def attention_out(place, tasks, counts, queries, plane, ends, mixed):
    return pl.pallas_call(
        local_gradients_kernel,
        out_shape=[HALF_BF16, HALF_F32, HALF_BF16],
        in_specs=[SMEM] * 3 + [VMEM] * 3 + [ANY],
        out_specs=[VMEM] * 3,
        scratch_shapes=[
            pltpu.VMEM((HALF, BLOCK, WIDTH), jnp.float32),
            pltpu.VMEM((PLANE, BLOCK, WIDTH), jnp.float32),
        ]
        + BOTHS
        + PAIRS
        + [pltpu.SemaphoreType.DMA],
        compiler_params=PARAMS,
        cost_estimate=cost(128),
        name="local_gradients",
    )(place, tasks, counts, queries, plane, ends, mixed)


def per_device(queries, key_rows, value_rows, cotangent, block_list):
    depth = lax.axis_size("z")
    core, x_hi, z = lax.axis_index("core"), lax.axis_index("x_hi"), lax.axis_index("z")
    place = jnp.stack([core, x_hi]).astype(jnp.int32)
    packed = pl.pallas_call(
        pack_kernel,
        out_shape=jax.ShapeDtypeStruct((PLANE, BLOCK, WIDTH), jnp.bfloat16),
        in_specs=[SMEM] + [ANY] * 4,
        out_specs=VMEM,
        scratch_shapes=[pltpu.VMEM(queries.shape, jnp.bfloat16)] * 4
        + [pltpu.SemaphoreType.DMA((PARTS, 4))],
        compiler_params=EDGE_PARAMS,
        name="pack",
    )(place, queries, key_rows, value_rows, cotangent)
    received = lax.all_to_all(packed, AXES, 0, 0, tiled=True)
    key_value = lax.dynamic_slice_in_dim(received, core * HALF, HALF, 0)
    query_grad_rows = lax.dynamic_slice_in_dim(received, (1 - core) * HALF, HALF, 0)
    mate = to_mate(key_value)
    halo = moved(
        key_value, ("z", "core"), lambda z, c: ((z + (1 if c else depth - 1)) % depth, c)
    )
    first_query = z * PLANE + (1 - core) * HALF
    first_key = z * PLANE - core * HALF
    listed = lax.dynamic_slice_in_dim(block_list, first_query, HALF, 0)
    own_blocks = first_query + jnp.arange(HALF, dtype=jnp.int32)
    alive = (jnp.arange(SLOTS)[None, :] == 0) | (listed != own_blocks[:, None])
    index = listed - first_key
    local_tasks, halo_tasks, counts, stats, plane = attention_in(
        place, index, alive.astype(jnp.int32), query_grad_rows, key_value, mate
    )
    ends, mixed, halo_part = attention_halo(halo_tasks, counts, query_grad_rows, halo, stats)
    halo_sum = moved(
        halo_part, ("z", "core"), lambda z, c: ((z + (depth - 1 if c else 1)) % depth, c)
    )
    query_out, own_part, mate_part = attention_out(
        place, local_tasks, counts, query_grad_rows, plane, ends, mixed
    )
    mate_sum = to_mate(mate_part)
    own_sum = pl.pallas_call(
        halo_sum_kernel,
        out_shape=HALF_F32,
        in_specs=[VMEM] * 2,
        out_specs=VMEM,
        compiler_params=PARAMS,
        name="halo_total",
    )(own_part, halo_sum)
    outgoing = pl.pallas_call(
        sum_kernel,
        out_shape=jax.ShapeDtypeStruct((PLANE, BLOCK, WIDTH), jnp.bfloat16),
        in_specs=[SMEM] + [VMEM] * 3,
        out_specs=VMEM,
        compiler_params=PARAMS,
        name="total",
    )(place, query_out, own_sum, mate_sum)
    returned = lax.all_to_all(outgoing, AXES, 0, 0, tiled=True)
    rows = jax.ShapeDtypeStruct(queries.shape, jnp.bfloat16)
    return pl.pallas_call(
        unpack_kernel,
        out_shape=[rows] * 4,
        in_specs=[SMEM, VMEM],
        out_specs=[ANY] * 4,
        scratch_shapes=[pltpu.VMEM(queries.shape, jnp.bfloat16)] * 4
        + [pltpu.SemaphoreType.DMA((PARTS, 4))],
        compiler_params=PARAMS,
        name="unpack",
    )(place, returned)


def solution(mesh):
    fine = Mesh(mesh.devices.reshape(2, 4, 16, 2, 2), ("x_lo", "y", "z", "x_hi", "core"))
    rows = P(("z", "x_hi", "core", "x_lo", "y"), None)
    return jax.shard_map(
        per_device,
        mesh=fine,
        in_specs=(rows,) * 4 + (P(),),
        out_specs=(rows,) * 4,
        check_vma=False,
    )
```

```python
import jax
import jax.numpy as jnp
import numpy as np
from jax import lax
from jax.experimental import pallas as pl
from jax.experimental.pallas import tpu as pltpu
from jax.sharding import Mesh, PartitionSpec as P

HEADS = 16
HEAD_SIZE = 64
BLOCK = 128
WIDTH = 2 * HEAD_SIZE
SCALING = HEAD_SIZE ** (-0.5)
PLANE = 32
HALF = PLANE // 2
SLOTS = 8
AXES = ("x_hi", "core", "x_lo", "y")
VMEM_LIMIT = 40 * 1024 * 1024
KEYS = SLOTS * BLOCK
CHUNK = 16
LANES = 128
PART = 256
PARTS = HEADS * HEAD_SIZE // PART


def lane_pair(left, right, odd):
    start = HEAD_SIZE if odd else 0
    return jnp.concatenate(
        [left[:, start : start + HEAD_SIZE], right[:, start : start + HEAD_SIZE]], axis=1
    )


def slot_of(head, core):
    return (head // 8) * 16 + core * 8 + head % 8


def pack_kernel(
    q_hbm, k_hbm, v_hbm, g_hbm, out_hbm, q_ref, k_ref, v_ref, g_ref, out_ref, in_sems, out_sems
):
    x_hi = lax.axis_index("x_hi")
    parts = [slice(p * PART, (p + 1) * PART) for p in range(PARTS)]
    arrivals = [
        [
            pltpu.make_async_copy(source.at[:, part], target.at[:, part], in_sems.at[p, n])
            for n, (source, target) in enumerate(
                ((k_hbm, k_ref), (v_hbm, v_ref), (q_hbm, q_ref), (g_hbm, g_ref))
            )
        ]
        for p, part in enumerate(parts)
    ]
    for group in arrivals:
        for copy in group:
            copy.start()
    departures = []
    for p in range(PARTS):
        for copy in arrivals[p]:
            copy.wait()
        heads = PART // HEAD_SIZE
        for head in range(p * heads, (p + 1) * heads):
            columns = slice(head // 2 * WIDTH, (head // 2 + 1) * WIDTH)
            out_ref[slot_of(head, x_hi)] = lane_pair(
                k_ref[:, columns], v_ref[:, columns], head % 2
            )
            out_ref[slot_of(head, 1 - x_hi)] = lane_pair(
                q_ref[:, columns], g_ref[:, columns], head % 2
            )
        for n in range(2):
            slots = pl.ds(slot_of(p * heads, n), heads)
            copy = pltpu.make_async_copy(out_ref.at[slots], out_hbm.at[slots], out_sems.at[p, n])
            copy.start()
            departures.append(copy)
    for copy in departures:
        copy.wait()


def unpack_kernel(
    in_ref, o_hbm, dq_hbm, dk_hbm, dv_hbm, o_ref, dq_ref, dk_ref, dv_ref, sems
):
    x_hi = lax.axis_index("x_hi")
    copies = []
    for pair in range(HEADS // 2):
        columns = slice(pair * WIDTH, (pair + 1) * WIDTH)
        even, odd = 2 * pair, 2 * pair + 1
        kv0, kv1 = in_ref[slot_of(even, x_hi)], in_ref[slot_of(odd, x_hi)]
        qo0, qo1 = in_ref[slot_of(even, 1 - x_hi)], in_ref[slot_of(odd, 1 - x_hi)]
        dk_ref[:, columns] = lane_pair(kv0, kv1, 0)
        dv_ref[:, columns] = lane_pair(kv0, kv1, 1)
        dq_ref[:, columns] = lane_pair(qo0, qo1, 0)
        o_ref[:, columns] = lane_pair(qo0, qo1, 1)
        if (pair + 1) * WIDTH % PART == 0:
            p = pair * WIDTH // PART
            part = slice(p * PART, (p + 1) * PART)
            for n, (source, target) in enumerate(
                ((o_ref, o_hbm), (dq_ref, dq_hbm), (dk_ref, dk_hbm), (dv_ref, dv_hbm))
            ):
                copy = pltpu.make_async_copy(source.at[:, part], target.at[:, part], sems.at[p, n])
                copy.start()
                copies.append(copy)
    for copy in copies:
        copy.wait()


def split_kernel(in_ref, kv_ref, qg_ref):
    core = lax.axis_index("core")
    kv_ref[...] = in_ref[pl.ds(core * HALF, HALF)]
    qg_ref[...] = in_ref[pl.ds((1 - core) * HALF, HALF)]


def attention_kernel(
    list_hbm, qg_ref, own_ref, mate_ref, halo_ref,
    qo_ref, own_out, mate_out, halo_out,
    window, accum, both_even, both_odd, pair_even, pair_odd, listed, table, sem,
):
    core, z = lax.axis_index("core"), lax.axis_index("z")
    own_at = 2 * core * HALF
    halo_at = 2 * HALF - own_at
    first_query = z * PLANE + (1 - core) * HALF
    first_key = z * PLANE - core * HALF
    lanes = listed.shape[1]
    at = lax.div(first_query, lanes) * lanes
    copy = pltpu.make_async_copy(
        list_hbm.at[:, pl.ds(pl.multiple_of(at, lanes), lanes)], listed, sem
    )
    copy.start()
    window[pl.ds(own_at, HALF)] = own_ref[...]
    window[HALF : 2 * HALF] = mate_ref[...]
    window[pl.ds(halo_at, HALF)] = halo_ref[...]
    accum[...] = jnp.zeros_like(accum)
    pair_odd[...] = jnp.zeros_like(pair_odd)
    copy.wait()

    def note(i, carry):
        for s in range(SLOTS):
            block = listed[s, first_query - at + i]
            dead = (block == first_query + i) if s else False
            table[i, s] = jnp.where(dead, -1, block - first_key)
        return carry

    lax.fori_loop(0, HALF, note, 0)

    def blocks_of(i):
        return [
            jnp.where(table[i, s] < 0, table[i, 0], table[i, s]) if s else table[i, 0]
            for s in range(SLOTS)
        ]

    left = lax.broadcasted_iota(jnp.int32, (BLOCK, WIDTH), 1) < HEAD_SIZE

    def listed_rows(i):
        return jnp.concatenate([window[b] for b in blocks_of(i)], axis=0)

    def query_rows(i):
        qg = qg_ref[i]
        zero = jnp.zeros_like(qg)
        return jnp.concatenate(
            [jnp.where(left, qg * jnp.bfloat16(SCALING), zero), jnp.where(left, zero, qg)], axis=0
        )

    def products(i, both):
        both[...] = lax.dot_general(
            query_rows(i), listed_rows(i), (((1,), (1,)), ((), ())),
            preferred_element_type=jnp.float32,
        )

    def weigh(i, both, pair):
        live = [table[i, s] >= 0 for s in range(SLOTS)]
        for r in range(0, BLOCK, CHUNK):
            scores = jnp.concatenate(
                [
                    jnp.where(live[s], both[r : r + CHUNK, s * BLOCK : (s + 1) * BLOCK], -jnp.inf)
                    for s in range(SLOTS)
                ],
                axis=1,
            )
            dprob = both[BLOCK + r : BLOCK + r + CHUNK]
            weights = jnp.exp(scores - jnp.max(scores, axis=1, keepdims=True))
            probs = weights * (1.0 / jnp.sum(weights, axis=1, keepdims=True))
            terms = probs * dprob
            dscore = terms - probs * jnp.sum(terms, axis=1, keepdims=True)
            pair[r : r + CHUNK] = dscore.astype(jnp.bfloat16)
            pair[BLOCK + r : BLOCK + r + CHUNK] = probs.astype(jnp.bfloat16)

    def results(i, pair):
        stacked = pair[...]
        mixed = jnp.dot(stacked, listed_rows(i), preferred_element_type=jnp.float32)
        qo_ref[i] = jnp.where(left, mixed[:BLOCK] * SCALING, mixed[BLOCK:]).astype(jnp.bfloat16)
        grads = lax.dot_general(
            stacked, query_rows(i), (((0,), (0,)), ((), ())), preferred_element_type=jnp.float32
        )
        for s, block in enumerate(blocks_of(i)):
            accum[block] += grads[s * BLOCK : (s + 1) * BLOCK]

    products(0, both_even)

    def step(j, carry):
        even, odd = 2 * j, 2 * j + 1
        products(odd, both_odd)
        weigh(even, both_even, pair_even)
        results(jnp.maximum(even - 1, 0), pair_odd)
        products(jnp.minimum(even + 2, HALF - 1), both_even)
        weigh(odd, both_odd, pair_odd)
        results(even, pair_even)
        return carry

    lax.fori_loop(0, HALF // 2, step, 0)
    results(HALF - 1, pair_odd)
    halo_out[...] = accum[pl.ds(halo_at, HALF)].astype(jnp.bfloat16)
    mate_out[...] = accum[HALF : 2 * HALF].astype(jnp.bfloat16)
    own_out[...] = accum[pl.ds(own_at, HALF)]


def halo_sum_kernel(own_ref, halo_ref, out_ref):
    out_ref[...] = own_ref[...] + halo_ref[...].astype(jnp.float32)


def sum_kernel(qo_ref, own_ref, mate_ref, out_ref):
    core = lax.axis_index("core")
    total = own_ref[...] + mate_ref[...].astype(jnp.float32)
    out_ref[pl.ds(core * HALF, HALF)] = total.astype(jnp.bfloat16)
    out_ref[pl.ds((1 - core) * HALF, HALF)] = qo_ref[...]


VMEM = pl.BlockSpec(memory_space=pltpu.VMEM)
ANY = pl.BlockSpec(memory_space=pl.ANY)
PARAMS = pltpu.CompilerParams(vmem_limit_bytes=VMEM_LIMIT)
EDGE_PARAMS = pltpu.CompilerParams(vmem_limit_bytes=60 * 1024 * 1024)


def moved(value, axes, target):
    sizes = [lax.axis_size(a) for a in axes]
    pairs = []
    for source in range(int(np.prod(sizes))):
        spot = [int(t) for t in np.unravel_index(source, sizes)]
        pairs.append((source, int(np.ravel_multi_index(target(*spot), sizes))))
    return lax.ppermute(value, axes, pairs)


def to_mate(value):
    return moved(value, ("core",), lambda c: (1 - c,))


def per_device(queries, key_rows, value_rows, cotangent, block_list):
    depth = lax.axis_size("z")
    plane = jax.ShapeDtypeStruct((PLANE, BLOCK, WIDTH), jnp.bfloat16)
    packed = pl.pallas_call(
        pack_kernel,
        out_shape=plane,
        in_specs=[ANY] * 4,
        out_specs=ANY,
        scratch_shapes=[pltpu.VMEM(queries.shape, jnp.bfloat16)] * 4
        + [
            pltpu.VMEM(plane.shape, jnp.bfloat16),
            pltpu.SemaphoreType.DMA((PARTS, 4)),
            pltpu.SemaphoreType.DMA((PARTS, 2)),
        ],
        compiler_params=EDGE_PARAMS,
        name="pack",
    )(queries, key_rows, value_rows, cotangent)
    received = lax.all_to_all(packed, AXES, 0, 0, tiled=True)
    half = (HALF, BLOCK, WIDTH)
    key_value, query_grad_rows = pl.pallas_call(
        split_kernel,
        out_shape=[jax.ShapeDtypeStruct(half, jnp.bfloat16)] * 2,
        in_specs=[VMEM],
        out_specs=[VMEM] * 2,
        compiler_params=PARAMS,
        name="split",
    )(received)
    mate = to_mate(key_value)
    halo = moved(
        key_value, ("z", "core"), lambda z, c: ((z + (1 if c else depth - 1)) % depth, c)
    )
    query_out, own_part, mate_part, halo_part = pl.pallas_call(
        attention_kernel,
        out_shape=[
            jax.ShapeDtypeStruct(half, jnp.bfloat16),
            jax.ShapeDtypeStruct(half, jnp.float32),
            jax.ShapeDtypeStruct(half, jnp.bfloat16),
            jax.ShapeDtypeStruct(half, jnp.bfloat16),
        ],
        in_specs=[ANY] + [VMEM] * 4,
        out_specs=[VMEM] * 4,
        scratch_shapes=[
            pltpu.VMEM((3 * HALF, BLOCK, WIDTH), jnp.bfloat16),
            pltpu.VMEM((3 * HALF, BLOCK, WIDTH), jnp.float32),
            pltpu.VMEM((2 * BLOCK, KEYS), jnp.float32),
            pltpu.VMEM((2 * BLOCK, KEYS), jnp.float32),
            pltpu.VMEM((2 * BLOCK, KEYS), jnp.bfloat16),
            pltpu.VMEM((2 * BLOCK, KEYS), jnp.bfloat16),
            pltpu.SMEM((SLOTS, LANES), jnp.int32),
            pltpu.SMEM((HALF, SLOTS), jnp.int32),
            pltpu.SemaphoreType.DMA,
        ],
        compiler_params=PARAMS,
        name="attention",
    )(block_list.T, query_grad_rows, key_value, mate, halo)
    mate_sum = to_mate(mate_part)
    halo_sum = moved(
        halo_part, ("z", "core"), lambda z, c: ((z + (depth - 1 if c else 1)) % depth, c)
    )
    own_sum = pl.pallas_call(
        halo_sum_kernel,
        out_shape=jax.ShapeDtypeStruct(half, jnp.float32),
        in_specs=[VMEM] * 2,
        out_specs=VMEM,
        compiler_params=PARAMS,
        name="halo_total",
    )(own_part, halo_sum)
    outgoing = pl.pallas_call(
        sum_kernel,
        out_shape=plane,
        in_specs=[VMEM] * 3,
        out_specs=VMEM,
        compiler_params=PARAMS,
        name="total",
    )(query_out, own_sum, mate_sum)
    returned = lax.all_to_all(outgoing, AXES, 0, 0, tiled=True)
    rows = jax.ShapeDtypeStruct(queries.shape, jnp.bfloat16)
    return pl.pallas_call(
        unpack_kernel,
        out_shape=[rows] * 4,
        in_specs=[VMEM],
        out_specs=[ANY] * 4,
        scratch_shapes=[pltpu.VMEM(queries.shape, jnp.bfloat16)] * 4
        + [pltpu.SemaphoreType.DMA((PARTS, 4))],
        compiler_params=PARAMS,
        name="unpack",
    )(returned)


def solution(mesh):
    fine = Mesh(mesh.devices.reshape(2, 4, 16, 2, 2), ("x_lo", "y", "z", "x_hi", "core"))
    rows = P(("z", "x_hi", "core", "x_lo", "y"), None)
    return jax.shard_map(
        per_device,
        mesh=fine,
        in_specs=(rows,) * 4 + (P(),),
        out_specs=(rows,) * 4,
        check_vma=False,
    )
```

```python
import jax
import jax.numpy as jnp
import numpy as np
from jax import lax
from jax.experimental import pallas as pl
from jax.experimental.pallas import tpu as pltpu
from jax.sharding import Mesh, PartitionSpec as P

HEADS = 16
HEAD_SIZE = 64
BLOCK = 128
WIDTH = 2 * HEAD_SIZE
SCALING = HEAD_SIZE ** (-0.5)
PLANE = 32
HALF = PLANE // 2
QUARTER = HALF // 2
SLOTS = 8
AXES = ("x_hi", "core", "x_lo", "y")
VMEM_LIMIT = 40 * 1024 * 1024
KEYS = SLOTS * BLOCK
CHUNK = 16
LANES = 128
PART = 256
PARTS = HEADS * HEAD_SIZE // PART


def lane_pair(left, right, odd):
    start = HEAD_SIZE if odd else 0
    return jnp.concatenate(
        [left[:, start : start + HEAD_SIZE], right[:, start : start + HEAD_SIZE]], axis=1
    )


def slot_of(head, core):
    return (head // 8) * 16 + core * 8 + head % 8


def pack_kernel(
    q_hbm, k_hbm, v_hbm, g_hbm, out_hbm, q_ref, k_ref, v_ref, g_ref, out_ref, in_sems, out_sems
):
    x_hi = lax.axis_index("x_hi")
    parts = [slice(p * PART, (p + 1) * PART) for p in range(PARTS)]
    arrivals = [
        [
            pltpu.make_async_copy(source.at[:, part], target.at[:, part], in_sems.at[p, n])
            for n, (source, target) in enumerate(
                ((k_hbm, k_ref), (v_hbm, v_ref), (q_hbm, q_ref), (g_hbm, g_ref))
            )
        ]
        for p, part in enumerate(parts)
    ]
    for group in arrivals:
        for copy in group:
            copy.start()
    departures = []
    for p in range(PARTS):
        for copy in arrivals[p]:
            copy.wait()
        heads = PART // HEAD_SIZE
        for head in range(p * heads, (p + 1) * heads):
            columns = slice(head // 2 * WIDTH, (head // 2 + 1) * WIDTH)
            out_ref[slot_of(head, x_hi)] = lane_pair(
                k_ref[:, columns], v_ref[:, columns], head % 2
            )
            out_ref[slot_of(head, 1 - x_hi)] = lane_pair(
                q_ref[:, columns], g_ref[:, columns], head % 2
            )
        for n in range(2):
            slots = pl.ds(slot_of(p * heads, n), heads)
            copy = pltpu.make_async_copy(out_ref.at[slots], out_hbm.at[slots], out_sems.at[p, n])
            copy.start()
            departures.append(copy)
    for copy in departures:
        copy.wait()


def unpack_kernel(
    in_ref, o_hbm, dq_hbm, dk_hbm, dv_hbm, o_ref, dq_ref, dk_ref, dv_ref, sems
):
    x_hi = lax.axis_index("x_hi")
    copies = []
    for pair in range(HEADS // 2):
        columns = slice(pair * WIDTH, (pair + 1) * WIDTH)
        even, odd = 2 * pair, 2 * pair + 1
        kv0, kv1 = in_ref[slot_of(even, x_hi)], in_ref[slot_of(odd, x_hi)]
        qo0, qo1 = in_ref[slot_of(even, 1 - x_hi)], in_ref[slot_of(odd, 1 - x_hi)]
        dk_ref[:, columns] = lane_pair(kv0, kv1, 0)
        dv_ref[:, columns] = lane_pair(kv0, kv1, 1)
        dq_ref[:, columns] = lane_pair(qo0, qo1, 0)
        o_ref[:, columns] = lane_pair(qo0, qo1, 1)
        if (pair + 1) * WIDTH % PART == 0:
            p = pair * WIDTH // PART
            part = slice(p * PART, (p + 1) * PART)
            for n, (source, target) in enumerate(
                ((o_ref, o_hbm), (dq_ref, dq_hbm), (dk_ref, dk_hbm), (dv_ref, dv_hbm))
            ):
                copy = pltpu.make_async_copy(source.at[:, part], target.at[:, part], sems.at[p, n])
                copy.start()
                copies.append(copy)
    for copy in copies:
        copy.wait()


def split_kernel(in_ref, kv_ref, qg_ref, near_ref, far_ref):
    core = lax.axis_index("core")
    kv_at = core * HALF
    kv_ref[...] = in_ref[pl.ds(kv_at, HALF)]
    qg_ref[...] = in_ref[pl.ds((1 - core) * HALF, HALF)]
    near_ref[...] = in_ref[pl.ds(kv_at + core * QUARTER, QUARTER)]
    far_ref[...] = in_ref[pl.ds(kv_at + (1 - core) * QUARTER, QUARTER)]


def near_kernel(list_hbm, qg_ref, own_ref, mate_ref, near_ref, qo_ref, sums, *scratch):
    sums[...] = jnp.zeros_like(sums)
    core = lax.axis_index("core")
    attend(core, list_hbm, qg_ref, own_ref, mate_ref, (near_ref,), qo_ref, sums, *scratch)


def far_kernel(
    list_hbm, qg_ref, own_ref, mate_ref, near_ref, far_ref, sums_ref,
    qo_ref, own_out, mate_out, halo_out, sums, *scratch,
):
    sums[...] = sums_ref[...]
    core = lax.axis_index("core")
    attend(
        1 - core, list_hbm, qg_ref, own_ref, mate_ref, (near_ref, far_ref), qo_ref, sums, *scratch
    )
    own_at = 2 * core * HALF
    halo_out[...] = sums[pl.ds(2 * HALF - own_at, HALF)].astype(jnp.bfloat16)
    mate_out[...] = sums[HALF : 2 * HALF].astype(jnp.bfloat16)
    own_out[...] = sums[pl.ds(own_at, HALF)]


def attend(
    group, list_hbm, qg_ref, own_ref, mate_ref, halo_refs, qo_ref, accum,
    window, both_even, both_odd, pair_even, pair_odd, listed, table, sem,
):
    core, z = lax.axis_index("core"), lax.axis_index("z")
    own_at = 2 * core * HALF
    halo_at = 2 * HALF - own_at
    first = group * QUARTER
    first_query = z * PLANE + (1 - core) * HALF + first
    first_key = z * PLANE - core * HALF
    lanes = listed.shape[1]
    at = lax.div(first_query, lanes) * lanes
    copy = pltpu.make_async_copy(
        list_hbm.at[:, pl.ds(pl.multiple_of(at, lanes), lanes)], listed, sem
    )
    copy.start()
    window[pl.ds(own_at, HALF)] = own_ref[...]
    window[HALF : 2 * HALF] = mate_ref[...]
    for side, halo_ref in zip((core, 1 - core), halo_refs):
        window[pl.ds(halo_at + side * QUARTER, QUARTER)] = halo_ref[...]
    pair_odd[...] = jnp.zeros_like(pair_odd)
    copy.wait()

    def note(i, carry):
        for s in range(SLOTS):
            block = listed[s, first_query - at + i]
            dead = (block == first_query + i) if s else False
            table[i, s] = jnp.where(dead, -1, block - first_key)
        return carry

    lax.fori_loop(0, QUARTER, note, 0)

    def blocks_of(i):
        return [
            jnp.where(table[i, s] < 0, table[i, 0], table[i, s]) if s else table[i, 0]
            for s in range(SLOTS)
        ]

    left = lax.broadcasted_iota(jnp.int32, (BLOCK, WIDTH), 1) < HEAD_SIZE

    def listed_rows(i):
        return jnp.concatenate([window[b] for b in blocks_of(i)], axis=0)

    def query_rows(i):
        qg = qg_ref[first + i]
        zero = jnp.zeros_like(qg)
        return jnp.concatenate(
            [jnp.where(left, qg * jnp.bfloat16(SCALING), zero), jnp.where(left, zero, qg)], axis=0
        )

    def products(i, both):
        both[...] = lax.dot_general(
            query_rows(i), listed_rows(i), (((1,), (1,)), ((), ())),
            preferred_element_type=jnp.float32,
        )

    def weigh(i, both, pair):
        live = [table[i, s] >= 0 for s in range(SLOTS)]
        for r in range(0, BLOCK, CHUNK):
            scores = jnp.concatenate(
                [
                    jnp.where(live[s], both[r : r + CHUNK, s * BLOCK : (s + 1) * BLOCK], -jnp.inf)
                    for s in range(SLOTS)
                ],
                axis=1,
            )
            dprob = both[BLOCK + r : BLOCK + r + CHUNK]
            weights = jnp.exp(scores - jnp.max(scores, axis=1, keepdims=True))
            probs = weights * (1.0 / jnp.sum(weights, axis=1, keepdims=True))
            terms = probs * dprob
            dscore = terms - probs * jnp.sum(terms, axis=1, keepdims=True)
            pair[r : r + CHUNK] = dscore.astype(jnp.bfloat16)
            pair[BLOCK + r : BLOCK + r + CHUNK] = probs.astype(jnp.bfloat16)

    def results(i, pair):
        stacked = pair[...]
        mixed = jnp.dot(stacked, listed_rows(i), preferred_element_type=jnp.float32)
        qo_ref[i] = jnp.where(left, mixed[:BLOCK] * SCALING, mixed[BLOCK:]).astype(jnp.bfloat16)
        grads = lax.dot_general(
            stacked, query_rows(i), (((0,), (0,)), ((), ())), preferred_element_type=jnp.float32
        )
        for s, block in enumerate(blocks_of(i)):
            accum[block] += grads[s * BLOCK : (s + 1) * BLOCK]

    products(0, both_even)

    def step(j, carry):
        even, odd = 2 * j, 2 * j + 1
        products(odd, both_odd)
        weigh(even, both_even, pair_even)
        results(jnp.maximum(even - 1, 0), pair_odd)
        products(jnp.minimum(even + 2, QUARTER - 1), both_even)
        weigh(odd, both_odd, pair_odd)
        results(even, pair_even)
        return carry

    lax.fori_loop(0, QUARTER // 2, step, 0)
    results(QUARTER - 1, pair_odd)


def halo_sum_kernel(own_ref, halo_ref, out_ref):
    out_ref[...] = own_ref[...] + halo_ref[...].astype(jnp.float32)


def sum_kernel(near_ref, far_ref, own_ref, mate_ref, out_ref):
    core = lax.axis_index("core")
    total = own_ref[...] + mate_ref[...].astype(jnp.float32)
    out_ref[pl.ds(core * HALF, HALF)] = total.astype(jnp.bfloat16)
    query_at = (1 - core) * HALF
    out_ref[pl.ds(query_at + core * QUARTER, QUARTER)] = near_ref[...]
    out_ref[pl.ds(query_at + (1 - core) * QUARTER, QUARTER)] = far_ref[...]


VMEM = pl.BlockSpec(memory_space=pltpu.VMEM)
ANY = pl.BlockSpec(memory_space=pl.ANY)
PARAMS = pltpu.CompilerParams(vmem_limit_bytes=VMEM_LIMIT)
EDGE_PARAMS = pltpu.CompilerParams(vmem_limit_bytes=60 * 1024 * 1024)


def moved(value, axes, target):
    sizes = [lax.axis_size(a) for a in axes]
    pairs = []
    for source in range(int(np.prod(sizes))):
        spot = [int(t) for t in np.unravel_index(source, sizes)]
        pairs.append((source, int(np.ravel_multi_index(target(*spot), sizes))))
    return lax.ppermute(value, axes, pairs)


def to_mate(value):
    return moved(value, ("core",), lambda c: (1 - c,))


def per_device(queries, key_rows, value_rows, cotangent, block_list):
    depth = lax.axis_size("z")
    plane = jax.ShapeDtypeStruct((PLANE, BLOCK, WIDTH), jnp.bfloat16)
    packed = pl.pallas_call(
        pack_kernel,
        out_shape=plane,
        in_specs=[ANY] * 4,
        out_specs=ANY,
        scratch_shapes=[pltpu.VMEM(queries.shape, jnp.bfloat16)] * 4
        + [
            pltpu.VMEM(plane.shape, jnp.bfloat16),
            pltpu.SemaphoreType.DMA((PARTS, 4)),
            pltpu.SemaphoreType.DMA((PARTS, 2)),
        ],
        compiler_params=EDGE_PARAMS,
        name="pack",
    )(queries, key_rows, value_rows, cotangent)
    received = lax.all_to_all(packed, AXES, 0, 0, tiled=True)
    half = (HALF, BLOCK, WIDTH)
    quarter = (QUARTER, BLOCK, WIDTH)
    sums = (3 * HALF, BLOCK, WIDTH)
    key_value, query_grad_rows, near_part, far_part = pl.pallas_call(
        split_kernel,
        out_shape=[jax.ShapeDtypeStruct(half, jnp.bfloat16)] * 2
        + [jax.ShapeDtypeStruct(quarter, jnp.bfloat16)] * 2,
        in_specs=[VMEM],
        out_specs=[VMEM] * 4,
        compiler_params=PARAMS,
        name="split",
    )(received)

    def inward(value):
        return moved(value, ("z", "core"), lambda z, c: ((z + (1 if c else depth - 1)) % depth, c))

    near = inward(near_part)
    mate = to_mate(key_value)
    far = inward(far_part)
    scratch = [
        pltpu.VMEM(sums, jnp.bfloat16),
        pltpu.VMEM((2 * BLOCK, KEYS), jnp.float32),
        pltpu.VMEM((2 * BLOCK, KEYS), jnp.float32),
        pltpu.VMEM((2 * BLOCK, KEYS), jnp.bfloat16),
        pltpu.VMEM((2 * BLOCK, KEYS), jnp.bfloat16),
        pltpu.SMEM((SLOTS, LANES), jnp.int32),
        pltpu.SMEM((QUARTER, SLOTS), jnp.int32),
        pltpu.SemaphoreType.DMA,
    ]
    work = pl.CostEstimate(
        flops=QUARTER * 6 * 2 * BLOCK * KEYS * WIDTH,
        bytes_accessed=1 << 20,
        transcendentals=QUARTER * BLOCK * KEYS,
    )
    query_near, near_sums = pl.pallas_call(
        near_kernel,
        out_shape=[
            jax.ShapeDtypeStruct(quarter, jnp.bfloat16),
            jax.ShapeDtypeStruct(sums, jnp.float32),
        ],
        in_specs=[ANY] + [VMEM] * 4,
        out_specs=[VMEM] * 2,
        scratch_shapes=scratch,
        compiler_params=PARAMS,
        cost_estimate=work,
        name="near",
    )(block_list.T, query_grad_rows, key_value, mate, near)
    query_far, own_part, mate_part, halo_part = pl.pallas_call(
        far_kernel,
        out_shape=[
            jax.ShapeDtypeStruct(quarter, jnp.bfloat16),
            jax.ShapeDtypeStruct(half, jnp.float32),
            jax.ShapeDtypeStruct(half, jnp.bfloat16),
            jax.ShapeDtypeStruct(half, jnp.bfloat16),
        ],
        in_specs=[ANY] + [VMEM] * 6,
        out_specs=[VMEM] * 4,
        scratch_shapes=[pltpu.VMEM(sums, jnp.float32)] + scratch,
        compiler_params=PARAMS,
        cost_estimate=work,
        name="far",
    )(block_list.T, query_grad_rows, key_value, mate, near, far, near_sums)
    mate_sum = to_mate(mate_part)
    halo_sum = moved(
        halo_part, ("z", "core"), lambda z, c: ((z + (depth - 1 if c else 1)) % depth, c)
    )
    own_sum = pl.pallas_call(
        halo_sum_kernel,
        out_shape=jax.ShapeDtypeStruct(half, jnp.float32),
        in_specs=[VMEM] * 2,
        out_specs=VMEM,
        compiler_params=PARAMS,
        name="halo_total",
    )(own_part, halo_sum)
    outgoing = pl.pallas_call(
        sum_kernel,
        out_shape=plane,
        in_specs=[VMEM] * 4,
        out_specs=VMEM,
        compiler_params=PARAMS,
        name="total",
    )(query_near, query_far, own_sum, mate_sum)
    returned = lax.all_to_all(outgoing, AXES, 0, 0, tiled=True)
    rows = jax.ShapeDtypeStruct(queries.shape, jnp.bfloat16)
    return pl.pallas_call(
        unpack_kernel,
        out_shape=[rows] * 4,
        in_specs=[VMEM],
        out_specs=[ANY] * 4,
        scratch_shapes=[pltpu.VMEM(queries.shape, jnp.bfloat16)] * 4
        + [pltpu.SemaphoreType.DMA((PARTS, 4))],
        compiler_params=PARAMS,
        name="unpack",
    )(returned)


def solution(mesh):
    fine = Mesh(mesh.devices.reshape(2, 4, 16, 2, 2), ("x_lo", "y", "z", "x_hi", "core"))
    rows = P(("z", "x_hi", "core", "x_lo", "y"), None)
    return jax.shard_map(
        per_device,
        mesh=fine,
        in_specs=(rows,) * 4 + (P(),),
        out_specs=(rows,) * 4,
        check_vma=False,
    )
```

```python
import jax
import jax.numpy as jnp
import numpy as np
from jax import lax
from jax.experimental import pallas as pl
from jax.experimental.pallas import tpu as pltpu
from jax.sharding import Mesh, PartitionSpec as P

HEADS = 16
HEAD_SIZE = 64
BLOCK = 128
WIDTH = 2 * HEAD_SIZE
SCALING = HEAD_SIZE ** (-0.5)
PLANE = 32
HALF = PLANE // 2
QUARTER = HALF // 2
SLOTS = 8
AXES = ("x_hi", "core", "x_lo", "y")
VMEM_LIMIT = 40 * 1024 * 1024
KEYS = SLOTS * BLOCK
CHUNK = 16
LANES = 128
PART = 256
PARTS = HEADS * HEAD_SIZE // PART


def lane_pair(left, right, odd):
    start = HEAD_SIZE if odd else 0
    return jnp.concatenate(
        [left[:, start : start + HEAD_SIZE], right[:, start : start + HEAD_SIZE]], axis=1
    )


def slot_of(head, core):
    return (head // 8) * 16 + core * 8 + head % 8


def pack_kernel(
    q_hbm, k_hbm, v_hbm, g_hbm, out_hbm, q_ref, k_ref, v_ref, g_ref, out_ref, in_sems, out_sems
):
    x_hi = lax.axis_index("x_hi")
    parts = [slice(p * PART, (p + 1) * PART) for p in range(PARTS)]
    arrivals = [
        [
            pltpu.make_async_copy(source.at[:, part], target.at[:, part], in_sems.at[p, n])
            for n, (source, target) in enumerate(
                ((k_hbm, k_ref), (v_hbm, v_ref), (q_hbm, q_ref), (g_hbm, g_ref))
            )
        ]
        for p, part in enumerate(parts)
    ]
    for group in arrivals:
        for copy in group:
            copy.start()
    departures = []
    for p in range(PARTS):
        for copy in arrivals[p]:
            copy.wait()
        heads = PART // HEAD_SIZE
        for head in range(p * heads, (p + 1) * heads):
            columns = slice(head // 2 * WIDTH, (head // 2 + 1) * WIDTH)
            out_ref[slot_of(head, x_hi)] = lane_pair(
                k_ref[:, columns], v_ref[:, columns], head % 2
            )
            out_ref[slot_of(head, 1 - x_hi)] = lane_pair(
                q_ref[:, columns], g_ref[:, columns], head % 2
            )
        for n in range(2):
            slots = pl.ds(slot_of(p * heads, n), heads)
            copy = pltpu.make_async_copy(out_ref.at[slots], out_hbm.at[slots], out_sems.at[p, n])
            copy.start()
            departures.append(copy)
    for copy in departures:
        copy.wait()


def unpack_kernel(
    in_ref, o_hbm, dq_hbm, dk_hbm, dv_hbm, o_ref, dq_ref, dk_ref, dv_ref, sems
):
    x_hi = lax.axis_index("x_hi")
    copies = []
    for pair in range(HEADS // 2):
        columns = slice(pair * WIDTH, (pair + 1) * WIDTH)
        even, odd = 2 * pair, 2 * pair + 1
        kv0, kv1 = in_ref[slot_of(even, x_hi)], in_ref[slot_of(odd, x_hi)]
        qo0, qo1 = in_ref[slot_of(even, 1 - x_hi)], in_ref[slot_of(odd, 1 - x_hi)]
        dk_ref[:, columns] = lane_pair(kv0, kv1, 0)
        dv_ref[:, columns] = lane_pair(kv0, kv1, 1)
        dq_ref[:, columns] = lane_pair(qo0, qo1, 0)
        o_ref[:, columns] = lane_pair(qo0, qo1, 1)
        if (pair + 1) * WIDTH % PART == 0:
            p = pair * WIDTH // PART
            part = slice(p * PART, (p + 1) * PART)
            for n, (source, target) in enumerate(
                ((o_ref, o_hbm), (dq_ref, dq_hbm), (dk_ref, dk_hbm), (dv_ref, dv_hbm))
            ):
                copy = pltpu.make_async_copy(source.at[:, part], target.at[:, part], sems.at[p, n])
                copy.start()
                copies.append(copy)
    for copy in copies:
        copy.wait()


def split_kernel(in_ref, kv_ref, qg_ref, near_ref, far_ref):
    core = lax.axis_index("core")
    kv_at = core * HALF
    kv_ref[...] = in_ref[pl.ds(kv_at, HALF)]
    qg_ref[...] = in_ref[pl.ds((1 - core) * HALF, HALF)]
    near_ref[...] = in_ref[pl.ds(kv_at + core * QUARTER, QUARTER)]
    far_ref[...] = in_ref[pl.ds(kv_at + (1 - core) * QUARTER, QUARTER)]


def copy_kernel(in_ref, out_ref):
    out_ref[...] = in_ref[...]


def near_kernel(list_hbm, qg_ref, own_ref, mate_ref, near_ref, qo_ref, sums, *scratch):
    sums[...] = jnp.zeros_like(sums)
    core = lax.axis_index("core")
    attend(core, list_hbm, qg_ref, own_ref, mate_ref, (near_ref,), qo_ref, sums, *scratch)


def far_kernel(
    list_hbm, qg_ref, own_ref, mate_ref, near_ref, far_ref, sums_ref,
    qo_ref, own_out, mate_out, halo_out, sums, *scratch,
):
    sums[...] = sums_ref[...]
    core = lax.axis_index("core")
    attend(
        1 - core, list_hbm, qg_ref, own_ref, mate_ref, (near_ref, far_ref), qo_ref, sums, *scratch
    )
    own_at = 2 * core * HALF
    halo_out[...] = sums[pl.ds(2 * HALF - own_at, HALF)].astype(jnp.bfloat16)
    mate_out[...] = sums[HALF : 2 * HALF].astype(jnp.bfloat16)
    own_out[...] = sums[pl.ds(own_at, HALF)]


def attend(
    group, list_hbm, qg_ref, own_ref, mate_ref, halo_refs, qo_ref, accum,
    window, both_even, both_odd, pair_even, pair_odd, listed, table, sem,
):
    core, z = lax.axis_index("core"), lax.axis_index("z")
    own_at = 2 * core * HALF
    halo_at = 2 * HALF - own_at
    first = group * QUARTER
    first_query = z * PLANE + (1 - core) * HALF + first
    first_key = z * PLANE - core * HALF
    lanes = listed.shape[1]
    at = lax.div(first_query, lanes) * lanes
    copy = pltpu.make_async_copy(
        list_hbm.at[:, pl.ds(pl.multiple_of(at, lanes), lanes)], listed, sem
    )
    copy.start()
    window[pl.ds(own_at, HALF)] = own_ref[...]
    window[HALF : 2 * HALF] = mate_ref[...]
    for side, halo_ref in zip((core, 1 - core), halo_refs):
        window[pl.ds(halo_at + side * QUARTER, QUARTER)] = halo_ref[...]
    pair_odd[...] = jnp.zeros_like(pair_odd)
    copy.wait()

    def note(i, carry):
        for s in range(SLOTS):
            block = listed[s, first_query - at + i]
            dead = (block == first_query + i) if s else False
            table[i, s] = jnp.where(dead, -1, block - first_key)
        return carry

    lax.fori_loop(0, QUARTER, note, 0)

    def blocks_of(i):
        return [
            jnp.where(table[i, s] < 0, table[i, 0], table[i, s]) if s else table[i, 0]
            for s in range(SLOTS)
        ]

    left = lax.broadcasted_iota(jnp.int32, (BLOCK, WIDTH), 1) < HEAD_SIZE

    def listed_rows(i):
        return jnp.concatenate([window[b] for b in blocks_of(i)], axis=0)

    def query_rows(i):
        qg = qg_ref[first + i]
        zero = jnp.zeros_like(qg)
        return jnp.concatenate(
            [jnp.where(left, qg * jnp.bfloat16(SCALING), zero), jnp.where(left, zero, qg)], axis=0
        )

    def products(i, both):
        both[...] = lax.dot_general(
            query_rows(i), listed_rows(i), (((1,), (1,)), ((), ())),
            preferred_element_type=jnp.float32,
        )

    def weigh(i, both, pair):
        live = [table[i, s] >= 0 for s in range(SLOTS)]
        for r in range(0, BLOCK, CHUNK):
            scores = jnp.concatenate(
                [
                    jnp.where(live[s], both[r : r + CHUNK, s * BLOCK : (s + 1) * BLOCK], -jnp.inf)
                    for s in range(SLOTS)
                ],
                axis=1,
            )
            dprob = both[BLOCK + r : BLOCK + r + CHUNK]
            weights = jnp.exp(scores - jnp.max(scores, axis=1, keepdims=True))
            probs = weights * (1.0 / jnp.sum(weights, axis=1, keepdims=True))
            terms = probs * dprob
            dscore = terms - probs * jnp.sum(terms, axis=1, keepdims=True)
            pair[r : r + CHUNK] = dscore.astype(jnp.bfloat16)
            pair[BLOCK + r : BLOCK + r + CHUNK] = probs.astype(jnp.bfloat16)

    def results(i, pair):
        stacked = pair[...]
        mixed = jnp.dot(stacked, listed_rows(i), preferred_element_type=jnp.float32)
        qo_ref[i] = jnp.where(left, mixed[:BLOCK] * SCALING, mixed[BLOCK:]).astype(jnp.bfloat16)
        grads = lax.dot_general(
            stacked, query_rows(i), (((0,), (0,)), ((), ())), preferred_element_type=jnp.float32
        )
        for s, block in enumerate(blocks_of(i)):
            accum[block] += grads[s * BLOCK : (s + 1) * BLOCK]

    products(0, both_even)

    def step(j, carry):
        even, odd = 2 * j, 2 * j + 1
        products(odd, both_odd)
        weigh(even, both_even, pair_even)
        results(jnp.maximum(even - 1, 0), pair_odd)
        products(jnp.minimum(even + 2, QUARTER - 1), both_even)
        weigh(odd, both_odd, pair_odd)
        results(even, pair_even)
        return carry

    lax.fori_loop(0, QUARTER // 2, step, 0)
    results(QUARTER - 1, pair_odd)


def halo_sum_kernel(own_ref, halo_ref, out_ref):
    out_ref[...] = own_ref[...] + halo_ref[...].astype(jnp.float32)


def sum_kernel(near_ref, far_ref, own_ref, mate_ref, out_ref):
    core = lax.axis_index("core")
    total = own_ref[...] + mate_ref[...].astype(jnp.float32)
    out_ref[pl.ds(core * HALF, HALF)] = total.astype(jnp.bfloat16)
    query_at = (1 - core) * HALF
    out_ref[pl.ds(query_at + core * QUARTER, QUARTER)] = near_ref[...]
    out_ref[pl.ds(query_at + (1 - core) * QUARTER, QUARTER)] = far_ref[...]


VMEM = pl.BlockSpec(memory_space=pltpu.VMEM)
ANY = pl.BlockSpec(memory_space=pl.ANY)
PARAMS = pltpu.CompilerParams(vmem_limit_bytes=VMEM_LIMIT)
EDGE_PARAMS = pltpu.CompilerParams(vmem_limit_bytes=60 * 1024 * 1024)


def moved(value, axes, target):
    sizes = [lax.axis_size(a) for a in axes]
    pairs = []
    for source in range(int(np.prod(sizes))):
        spot = [int(t) for t in np.unravel_index(source, sizes)]
        pairs.append((source, int(np.ravel_multi_index(target(*spot), sizes))))
    return lax.ppermute(value, axes, pairs)


def to_mate(value):
    return moved(value, ("core",), lambda c: (1 - c,))


def per_device(queries, key_rows, value_rows, cotangent, block_list):
    depth = lax.axis_size("z")
    plane = jax.ShapeDtypeStruct((PLANE, BLOCK, WIDTH), jnp.bfloat16)
    packed = pl.pallas_call(
        pack_kernel,
        out_shape=plane,
        in_specs=[ANY] * 4,
        out_specs=ANY,
        scratch_shapes=[pltpu.VMEM(queries.shape, jnp.bfloat16)] * 4
        + [
            pltpu.VMEM(plane.shape, jnp.bfloat16),
            pltpu.SemaphoreType.DMA((PARTS, 4)),
            pltpu.SemaphoreType.DMA((PARTS, 2)),
        ],
        compiler_params=EDGE_PARAMS,
        name="pack",
    )(queries, key_rows, value_rows, cotangent)
    received = lax.all_to_all(packed, AXES, 0, 0, tiled=True)
    half = (HALF, BLOCK, WIDTH)
    quarter = (QUARTER, BLOCK, WIDTH)
    sums = (3 * HALF, BLOCK, WIDTH)
    key_value, query_grad_rows, near_part, far_part = pl.pallas_call(
        split_kernel,
        out_shape=[jax.ShapeDtypeStruct(half, jnp.bfloat16)] * 2
        + [jax.ShapeDtypeStruct(quarter, jnp.bfloat16)] * 2,
        in_specs=[VMEM],
        out_specs=[VMEM] * 4,
        compiler_params=PARAMS,
        name="split",
    )(received)

    def inward(value):
        return moved(value, ("z", "core"), lambda z, c: ((z + (1 if c else depth - 1)) % depth, c))

    near = pl.pallas_call(
        copy_kernel,
        out_shape=jax.ShapeDtypeStruct(quarter, jnp.bfloat16),
        in_specs=[VMEM],
        out_specs=VMEM,
        compiler_params=PARAMS,
        cost_estimate=pl.CostEstimate(flops=1 << 32, bytes_accessed=1 << 20, transcendentals=0),
        name="near_copy",
    )(inward(near_part))
    mate = to_mate(key_value)
    far = inward(far_part)
    scratch = [
        pltpu.VMEM(sums, jnp.bfloat16),
        pltpu.VMEM((2 * BLOCK, KEYS), jnp.float32),
        pltpu.VMEM((2 * BLOCK, KEYS), jnp.float32),
        pltpu.VMEM((2 * BLOCK, KEYS), jnp.bfloat16),
        pltpu.VMEM((2 * BLOCK, KEYS), jnp.bfloat16),
        pltpu.SMEM((SLOTS, LANES), jnp.int32),
        pltpu.SMEM((QUARTER, SLOTS), jnp.int32),
        pltpu.SemaphoreType.DMA,
    ]
    work = pl.CostEstimate(
        flops=QUARTER * 6 * 2 * BLOCK * KEYS * WIDTH,
        bytes_accessed=1 << 20,
        transcendentals=QUARTER * BLOCK * KEYS,
    )
    query_near, near_sums = pl.pallas_call(
        near_kernel,
        out_shape=[
            jax.ShapeDtypeStruct(quarter, jnp.bfloat16),
            jax.ShapeDtypeStruct(sums, jnp.float32),
        ],
        in_specs=[ANY] + [VMEM] * 4,
        out_specs=[VMEM] * 2,
        scratch_shapes=scratch,
        compiler_params=PARAMS,
        cost_estimate=work,
        name="near",
    )(block_list.T, query_grad_rows, key_value, mate, near)
    query_far, own_part, mate_part, halo_part = pl.pallas_call(
        far_kernel,
        out_shape=[
            jax.ShapeDtypeStruct(quarter, jnp.bfloat16),
            jax.ShapeDtypeStruct(half, jnp.float32),
            jax.ShapeDtypeStruct(half, jnp.bfloat16),
            jax.ShapeDtypeStruct(half, jnp.bfloat16),
        ],
        in_specs=[ANY] + [VMEM] * 6,
        out_specs=[VMEM] * 4,
        scratch_shapes=[pltpu.VMEM(sums, jnp.float32)] + scratch,
        compiler_params=PARAMS,
        cost_estimate=work,
        name="far",
    )(block_list.T, query_grad_rows, key_value, mate, near, far, near_sums)
    mate_sum = to_mate(mate_part)
    halo_sum = moved(
        halo_part, ("z", "core"), lambda z, c: ((z + (depth - 1 if c else 1)) % depth, c)
    )
    own_sum = pl.pallas_call(
        halo_sum_kernel,
        out_shape=jax.ShapeDtypeStruct(half, jnp.float32),
        in_specs=[VMEM] * 2,
        out_specs=VMEM,
        compiler_params=PARAMS,
        name="halo_total",
    )(own_part, halo_sum)
    outgoing = pl.pallas_call(
        sum_kernel,
        out_shape=plane,
        in_specs=[VMEM] * 4,
        out_specs=VMEM,
        compiler_params=PARAMS,
        name="total",
    )(query_near, query_far, own_sum, mate_sum)
    returned = lax.all_to_all(outgoing, AXES, 0, 0, tiled=True)
    rows = jax.ShapeDtypeStruct(queries.shape, jnp.bfloat16)
    return pl.pallas_call(
        unpack_kernel,
        out_shape=[rows] * 4,
        in_specs=[VMEM],
        out_specs=[ANY] * 4,
        scratch_shapes=[pltpu.VMEM(queries.shape, jnp.bfloat16)] * 4
        + [pltpu.SemaphoreType.DMA((PARTS, 4))],
        compiler_params=PARAMS,
        name="unpack",
    )(returned)


def solution(mesh):
    fine = Mesh(mesh.devices.reshape(2, 4, 16, 2, 2), ("x_lo", "y", "z", "x_hi", "core"))
    rows = P(("z", "x_hi", "core", "x_lo", "y"), None)
    return jax.shard_map(
        per_device,
        mesh=fine,
        in_specs=(rows,) * 4 + (P(),),
        out_specs=(rows,) * 4,
        check_vma=False,
    )
```

```python
import jax
import jax.numpy as jnp
import numpy as np
from jax import lax
from jax.experimental import pallas as pl
from jax.experimental.pallas import tpu as pltpu
from jax.sharding import Mesh, PartitionSpec as P

HEADS = 16
HEAD_SIZE = 64
BLOCK = 128
WIDTH = 2 * HEAD_SIZE
SCALING = HEAD_SIZE ** (-0.5)
PLANE = 32
HALF = PLANE // 2
QUARTER = HALF // 2
SLOTS = 8
AXES = ("x_hi", "core", "x_lo", "y")
VMEM_LIMIT = 40 * 1024 * 1024
KEYS = SLOTS * BLOCK
CHUNK = 16
PIECES = 4
SPAN = KEYS // PIECES
PAIR = SLOTS // PIECES
LANES = 128
PART = 256
PARTS = HEADS * HEAD_SIZE // PART


def lane_pair(left, right, odd):
    start = HEAD_SIZE if odd else 0
    return jnp.concatenate(
        [left[:, start : start + HEAD_SIZE], right[:, start : start + HEAD_SIZE]], axis=1
    )


def turned_pair(left, right, odd):
    start = HEAD_SIZE if odd else 0
    return jnp.concatenate(
        [left[start : start + HEAD_SIZE], right[start : start + HEAD_SIZE]], axis=0
    ).T


def slot_of(head, core):
    return (head // 8) * 16 + core * 8 + head % 8


def pack_kernel(
    q_hbm, k_hbm, v_hbm, g_hbm, out_hbm, q_ref, k_ref, v_ref, g_ref, out_ref, in_sems, out_sems
):
    x_hi = lax.axis_index("x_hi")
    parts = [slice(p * PART, (p + 1) * PART) for p in range(PARTS)]
    arrivals = [
        [
            pltpu.make_async_copy(source.at[:, part], target.at[:, part], in_sems.at[p, n])
            for n, (source, target) in enumerate(
                ((k_hbm, k_ref), (v_hbm, v_ref), (q_hbm, q_ref), (g_hbm, g_ref))
            )
        ]
        for p, part in enumerate(parts)
    ]
    for group in arrivals:
        for copy in group:
            copy.start()
    departures = []
    for p in range(PARTS):
        for copy in arrivals[p]:
            copy.wait()
        heads = PART // HEAD_SIZE
        for head in range(p * heads, (p + 1) * heads):
            columns = slice(head // 2 * WIDTH, (head // 2 + 1) * WIDTH)
            out_ref[slot_of(head, x_hi)] = lane_pair(
                k_ref[:, columns], v_ref[:, columns], head % 2
            )
            out_ref[slot_of(head, 1 - x_hi)] = lane_pair(
                q_ref[:, columns], g_ref[:, columns], head % 2
            )
        for n in range(2):
            slots = pl.ds(slot_of(p * heads, n), heads)
            copy = pltpu.make_async_copy(out_ref.at[slots], out_hbm.at[slots], out_sems.at[p, n])
            copy.start()
            departures.append(copy)
    for copy in departures:
        copy.wait()


def unpack_kernel(
    in_ref, o_hbm, dq_hbm, dk_hbm, dv_hbm, o_ref, dq_ref, dk_ref, dv_ref, sems
):
    x_hi = lax.axis_index("x_hi")
    copies = []
    for pair in range(HEADS // 2):
        columns = slice(pair * WIDTH, (pair + 1) * WIDTH)
        even, odd = 2 * pair, 2 * pair + 1
        kv0, kv1 = in_ref[slot_of(even, x_hi)], in_ref[slot_of(odd, x_hi)]
        qo0, qo1 = in_ref[slot_of(even, 1 - x_hi)], in_ref[slot_of(odd, 1 - x_hi)]
        dk_ref[:, columns] = turned_pair(kv0, kv1, 0)
        dv_ref[:, columns] = turned_pair(kv0, kv1, 1)
        dq_ref[:, columns] = lane_pair(qo0, qo1, 0)
        o_ref[:, columns] = lane_pair(qo0, qo1, 1)
        if (pair + 1) * WIDTH % PART == 0:
            p = pair * WIDTH // PART
            part = slice(p * PART, (p + 1) * PART)
            for n, (source, target) in enumerate(
                ((o_ref, o_hbm), (dq_ref, dq_hbm), (dk_ref, dk_hbm), (dv_ref, dv_hbm))
            ):
                copy = pltpu.make_async_copy(source.at[:, part], target.at[:, part], sems.at[p, n])
                copy.start()
                copies.append(copy)
    for copy in copies:
        copy.wait()


def split_kernel(in_ref, kv_ref, qg_ref, near_ref, far_ref):
    core = lax.axis_index("core")
    kv_at = core * HALF
    kv_ref[...] = in_ref[pl.ds(kv_at, HALF)]
    qg_ref[...] = in_ref[pl.ds((1 - core) * HALF, HALF)]
    near_ref[...] = in_ref[pl.ds(kv_at + core * QUARTER, QUARTER)]
    far_ref[...] = in_ref[pl.ds(kv_at + (1 - core) * QUARTER, QUARTER)]


def copy_kernel(in_ref, out_ref):
    out_ref[...] = in_ref[...]


def near_kernel(list_hbm, qg_ref, own_ref, mate_ref, near_ref, qo_ref, sums, *scratch):
    sums[...] = jnp.zeros_like(sums)
    core = lax.axis_index("core")
    attend(core, list_hbm, qg_ref, own_ref, mate_ref, (near_ref,), qo_ref, sums, *scratch)


def far_kernel(
    list_hbm, qg_ref, own_ref, mate_ref, near_ref, far_ref, sums_ref,
    qo_ref, own_out, mate_out, halo_out, sums, *scratch,
):
    sums[...] = sums_ref[...]
    core = lax.axis_index("core")
    attend(
        1 - core, list_hbm, qg_ref, own_ref, mate_ref, (near_ref, far_ref), qo_ref, sums, *scratch
    )
    own_at = 2 * core * HALF
    halo_out[...] = sums[pl.ds(2 * HALF - own_at, HALF)].astype(jnp.bfloat16)
    mate_out[...] = sums[HALF : 2 * HALF].astype(jnp.bfloat16)
    own_out[...] = sums[pl.ds(own_at, HALF)]


def attend(
    group, list_hbm, qg_ref, own_ref, mate_ref, halo_refs, qo_ref, accum,
    window, both_even, both_odd, pair_even, pair_odd, listed, table, sem,
):
    core, z = lax.axis_index("core"), lax.axis_index("z")
    own_at = 2 * core * HALF
    halo_at = 2 * HALF - own_at
    first = group * QUARTER
    first_query = z * PLANE + (1 - core) * HALF + first
    first_key = z * PLANE - core * HALF
    lanes = listed.shape[1]
    at = lax.div(first_query, lanes) * lanes
    copy = pltpu.make_async_copy(
        list_hbm.at[:, pl.ds(pl.multiple_of(at, lanes), lanes)], listed, sem
    )
    copy.start()
    window[pl.ds(own_at, HALF)] = own_ref[...]
    window[HALF : 2 * HALF] = mate_ref[...]
    for side, halo_ref in zip((core, 1 - core), halo_refs):
        window[pl.ds(halo_at + side * QUARTER, QUARTER)] = halo_ref[...]
    pair_odd[...] = jnp.zeros_like(pair_odd)
    copy.wait()

    def note(i, carry):
        for s in range(SLOTS):
            block = listed[s, first_query - at + i]
            dead = (block == first_query + i) if s else False
            table[i, s] = jnp.where(dead, -1, block - first_key)
        return carry

    lax.fori_loop(0, QUARTER, note, 0)

    def blocks_of(i):
        return [
            jnp.where(table[i, s] < 0, table[i, 0], table[i, s]) if s else table[i, 0]
            for s in range(SLOTS)
        ]

    left = lax.broadcasted_iota(jnp.int32, (BLOCK, WIDTH), 1) < HEAD_SIZE

    def query_rows(i):
        qg = qg_ref[first + i]
        zero = jnp.zeros_like(qg)
        return jnp.concatenate(
            [jnp.where(left, qg * jnp.bfloat16(SCALING), zero), jnp.where(left, zero, qg)], axis=0
        )

    top = lax.broadcasted_iota(jnp.int32, (WIDTH, BLOCK), 0) < HEAD_SIZE

    def query_columns(i):
        columns = qg_ref[first + i].T
        zero = jnp.zeros_like(columns)
        return jnp.concatenate(
            [jnp.where(top, columns * jnp.bfloat16(SCALING), zero), jnp.where(top, zero, columns)],
            axis=1,
        )

    def products(i, both):
        rows, blocks = query_rows(i), blocks_of(i)
        for k in range(PIECES):
            kv = jnp.concatenate([window[b] for b in blocks[k * PAIR : (k + 1) * PAIR]], axis=0)
            both[:, k * SPAN : (k + 1) * SPAN] = lax.dot_general(
                rows, kv, (((1,), (1,)), ((), ())), preferred_element_type=jnp.float32
            )
            yield

    def weigh(i, both, pair):
        live = [table[i, s] >= 0 for s in range(SLOTS)]
        for r in range(0, BLOCK, CHUNK):
            scores = jnp.concatenate(
                [
                    jnp.where(live[s], both[r : r + CHUNK, s * BLOCK : (s + 1) * BLOCK], -jnp.inf)
                    for s in range(SLOTS)
                ],
                axis=1,
            )
            dprob = both[BLOCK + r : BLOCK + r + CHUNK]
            weights = jnp.exp(scores - jnp.max(scores, axis=1, keepdims=True))
            probs = weights * (1.0 / jnp.sum(weights, axis=1, keepdims=True))
            terms = probs * dprob
            dscore = terms - probs * jnp.sum(terms, axis=1, keepdims=True)
            pair[r : r + CHUNK] = dscore.astype(jnp.bfloat16)
            pair[BLOCK + r : BLOCK + r + CHUNK] = probs.astype(jnp.bfloat16)
            if (r // CHUNK + 1) % (BLOCK // CHUNK // PIECES) == 0:
                yield

    def results(i, pair):
        blocks = blocks_of(i)
        columns = query_columns(i)
        mixed = None
        for k in range(PIECES):
            stacked = pair[:, k * SPAN : (k + 1) * SPAN]
            here = blocks[k * PAIR : (k + 1) * PAIR]
            kv = jnp.concatenate([window[b] for b in here], axis=0)
            part = jnp.dot(stacked, kv, preferred_element_type=jnp.float32)
            mixed = part if mixed is None else mixed + part
            grads = jnp.dot(columns, stacked, preferred_element_type=jnp.float32)
            for s, block in enumerate(here):
                accum[block] += grads[:, s * BLOCK : (s + 1) * BLOCK]
            if k == PIECES - 1:
                qo_ref[i] = jnp.where(left, mixed[:BLOCK] * SCALING, mixed[BLOCK:]).astype(
                    jnp.bfloat16
                )
            yield

    def beside(*stages):
        for _ in zip(*stages):
            pass

    beside(products(0, both_even))

    def step(j, carry):
        even, odd = 2 * j, 2 * j + 1
        beside(
            products(odd, both_odd),
            weigh(even, both_even, pair_even),
            results(jnp.maximum(even - 1, 0), pair_odd),
        )
        beside(
            products(jnp.minimum(even + 2, QUARTER - 1), both_even),
            weigh(odd, both_odd, pair_odd),
            results(even, pair_even),
        )
        return carry

    lax.fori_loop(0, QUARTER // 2, step, 0)
    beside(results(QUARTER - 1, pair_odd))


def halo_sum_kernel(own_ref, halo_ref, out_ref):
    out_ref[...] = own_ref[...] + halo_ref[...].astype(jnp.float32)


def sum_kernel(near_ref, far_ref, own_ref, mate_ref, out_ref):
    core = lax.axis_index("core")
    total = own_ref[...] + mate_ref[...].astype(jnp.float32)
    out_ref[pl.ds(core * HALF, HALF)] = total.astype(jnp.bfloat16)
    query_at = (1 - core) * HALF
    out_ref[pl.ds(query_at + core * QUARTER, QUARTER)] = near_ref[...]
    out_ref[pl.ds(query_at + (1 - core) * QUARTER, QUARTER)] = far_ref[...]


VMEM = pl.BlockSpec(memory_space=pltpu.VMEM)
ANY = pl.BlockSpec(memory_space=pl.ANY)
PARAMS = pltpu.CompilerParams(vmem_limit_bytes=VMEM_LIMIT)
EDGE_PARAMS = pltpu.CompilerParams(vmem_limit_bytes=60 * 1024 * 1024)


def moved(value, axes, target):
    sizes = [lax.axis_size(a) for a in axes]
    pairs = []
    for source in range(int(np.prod(sizes))):
        spot = [int(t) for t in np.unravel_index(source, sizes)]
        pairs.append((source, int(np.ravel_multi_index(target(*spot), sizes))))
    return lax.ppermute(value, axes, pairs)


def to_mate(value):
    return moved(value, ("core",), lambda c: (1 - c,))


def per_device(queries, key_rows, value_rows, cotangent, block_list):
    depth = lax.axis_size("z")
    plane = jax.ShapeDtypeStruct((PLANE, BLOCK, WIDTH), jnp.bfloat16)
    packed = pl.pallas_call(
        pack_kernel,
        out_shape=plane,
        in_specs=[ANY] * 4,
        out_specs=ANY,
        scratch_shapes=[pltpu.VMEM(queries.shape, jnp.bfloat16)] * 4
        + [
            pltpu.VMEM(plane.shape, jnp.bfloat16),
            pltpu.SemaphoreType.DMA((PARTS, 4)),
            pltpu.SemaphoreType.DMA((PARTS, 2)),
        ],
        compiler_params=EDGE_PARAMS,
        name="pack",
    )(queries, key_rows, value_rows, cotangent)
    received = lax.all_to_all(packed, AXES, 0, 0, tiled=True)
    half = (HALF, BLOCK, WIDTH)
    quarter = (QUARTER, BLOCK, WIDTH)
    sums = (3 * HALF, BLOCK, WIDTH)
    key_value, query_grad_rows, near_part, far_part = pl.pallas_call(
        split_kernel,
        out_shape=[jax.ShapeDtypeStruct(half, jnp.bfloat16)] * 2
        + [jax.ShapeDtypeStruct(quarter, jnp.bfloat16)] * 2,
        in_specs=[VMEM],
        out_specs=[VMEM] * 4,
        compiler_params=PARAMS,
        name="split",
    )(received)

    def inward(value):
        return moved(value, ("z", "core"), lambda z, c: ((z + (1 if c else depth - 1)) % depth, c))

    near = pl.pallas_call(
        copy_kernel,
        out_shape=jax.ShapeDtypeStruct(quarter, jnp.bfloat16),
        in_specs=[VMEM],
        out_specs=VMEM,
        compiler_params=PARAMS,
        cost_estimate=pl.CostEstimate(flops=1 << 32, bytes_accessed=1 << 20, transcendentals=0),
        name="near_copy",
    )(inward(near_part))
    mate = to_mate(key_value)
    far = inward(far_part)
    scratch = [
        pltpu.VMEM(sums, jnp.bfloat16),
        pltpu.VMEM((2 * BLOCK, KEYS), jnp.float32),
        pltpu.VMEM((2 * BLOCK, KEYS), jnp.float32),
        pltpu.VMEM((2 * BLOCK, KEYS), jnp.bfloat16),
        pltpu.VMEM((2 * BLOCK, KEYS), jnp.bfloat16),
        pltpu.SMEM((SLOTS, LANES), jnp.int32),
        pltpu.SMEM((QUARTER, SLOTS), jnp.int32),
        pltpu.SemaphoreType.DMA,
    ]
    work = pl.CostEstimate(
        flops=QUARTER * 6 * 2 * BLOCK * KEYS * WIDTH,
        bytes_accessed=1 << 20,
        transcendentals=QUARTER * BLOCK * KEYS,
    )
    query_near, near_sums = pl.pallas_call(
        near_kernel,
        out_shape=[
            jax.ShapeDtypeStruct(quarter, jnp.bfloat16),
            jax.ShapeDtypeStruct(sums, jnp.float32),
        ],
        in_specs=[ANY] + [VMEM] * 4,
        out_specs=[VMEM] * 2,
        scratch_shapes=scratch,
        compiler_params=PARAMS,
        cost_estimate=work,
        name="near",
    )(block_list.T, query_grad_rows, key_value, mate, near)
    query_far, own_part, mate_part, halo_part = pl.pallas_call(
        far_kernel,
        out_shape=[
            jax.ShapeDtypeStruct(quarter, jnp.bfloat16),
            jax.ShapeDtypeStruct(half, jnp.float32),
            jax.ShapeDtypeStruct(half, jnp.bfloat16),
            jax.ShapeDtypeStruct(half, jnp.bfloat16),
        ],
        in_specs=[ANY] + [VMEM] * 6,
        out_specs=[VMEM] * 4,
        scratch_shapes=[pltpu.VMEM(sums, jnp.float32)] + scratch,
        compiler_params=PARAMS,
        cost_estimate=work,
        name="far",
    )(block_list.T, query_grad_rows, key_value, mate, near, far, near_sums)
    mate_sum = to_mate(mate_part)
    halo_sum = moved(
        halo_part, ("z", "core"), lambda z, c: ((z + (depth - 1 if c else 1)) % depth, c)
    )
    own_sum = pl.pallas_call(
        halo_sum_kernel,
        out_shape=jax.ShapeDtypeStruct(half, jnp.float32),
        in_specs=[VMEM] * 2,
        out_specs=VMEM,
        compiler_params=PARAMS,
        name="halo_total",
    )(own_part, halo_sum)
    outgoing = pl.pallas_call(
        sum_kernel,
        out_shape=plane,
        in_specs=[VMEM] * 4,
        out_specs=VMEM,
        compiler_params=PARAMS,
        name="total",
    )(query_near, query_far, own_sum, mate_sum)
    returned = lax.all_to_all(outgoing, AXES, 0, 0, tiled=True)
    rows = jax.ShapeDtypeStruct(queries.shape, jnp.bfloat16)
    return pl.pallas_call(
        unpack_kernel,
        out_shape=[rows] * 4,
        in_specs=[VMEM],
        out_specs=[ANY] * 4,
        scratch_shapes=[pltpu.VMEM(queries.shape, jnp.bfloat16)] * 4
        + [pltpu.SemaphoreType.DMA((PARTS, 4))],
        compiler_params=PARAMS,
        name="unpack",
    )(returned)


def solution(mesh):
    fine = Mesh(mesh.devices.reshape(2, 4, 16, 2, 2), ("x_lo", "y", "z", "x_hi", "core"))
    rows = P(("z", "x_hi", "core", "x_lo", "y"), None)
    return jax.shard_map(
        per_device,
        mesh=fine,
        in_specs=(rows,) * 4 + (P(),),
        out_specs=(rows,) * 4,
        check_vma=False,
    )
```

```python
import jax
import jax.numpy as jnp
import numpy as np
from jax import lax
from jax.experimental import pallas as pl
from jax.experimental.pallas import tpu as pltpu
from jax.sharding import Mesh, PartitionSpec as P

HEADS = 16
HEAD_SIZE = 64
BLOCK = 128
WIDTH = 2 * HEAD_SIZE
SCALING = HEAD_SIZE ** (-0.5)
PLANE = 32
HALF = PLANE // 2
QUARTER = HALF // 2
SLOTS = 8
AXES = ("x_hi", "core", "x_lo", "y")
VMEM_LIMIT = 40 * 1024 * 1024
KEYS = SLOTS * BLOCK
CHUNK = 16
PIECES = 4
SPAN = KEYS // PIECES
PAIR = SLOTS // PIECES
LANES = 128
PART = 256
PARTS = HEADS * HEAD_SIZE // PART


def lane_pair(left, right, odd):
    start = HEAD_SIZE if odd else 0
    return jnp.concatenate(
        [left[:, start : start + HEAD_SIZE], right[:, start : start + HEAD_SIZE]], axis=1
    )


def turned_pair(left, right, odd):
    start = HEAD_SIZE if odd else 0
    return jnp.concatenate(
        [left[start : start + HEAD_SIZE], right[start : start + HEAD_SIZE]], axis=0
    ).T


def slot_of(head, core):
    return (head // 8) * 16 + core * 8 + head % 8


def pack_kernel(
    q_hbm, k_hbm, v_hbm, g_hbm, out_hbm, q_ref, k_ref, v_ref, g_ref, out_ref, in_sems, out_sems
):
    x_hi = lax.axis_index("x_hi")
    parts = [slice(p * PART, (p + 1) * PART) for p in range(PARTS)]
    arrivals = [
        [
            pltpu.make_async_copy(source.at[:, part], target.at[:, part], in_sems.at[p, n])
            for n, (source, target) in enumerate(
                ((k_hbm, k_ref), (v_hbm, v_ref), (q_hbm, q_ref), (g_hbm, g_ref))
            )
        ]
        for p, part in enumerate(parts)
    ]
    for group in arrivals:
        for copy in group:
            copy.start()
    departures = []
    for p in range(PARTS):
        for copy in arrivals[p]:
            copy.wait()
        heads = PART // HEAD_SIZE
        for head in range(p * heads, (p + 1) * heads):
            columns = slice(head // 2 * WIDTH, (head // 2 + 1) * WIDTH)
            out_ref[slot_of(head, x_hi)] = lane_pair(
                k_ref[:, columns], v_ref[:, columns], head % 2
            )
            out_ref[slot_of(head, 1 - x_hi)] = lane_pair(
                q_ref[:, columns], g_ref[:, columns], head % 2
            )
        for n in range(2):
            slots = pl.ds(slot_of(p * heads, n), heads)
            copy = pltpu.make_async_copy(out_ref.at[slots], out_hbm.at[slots], out_sems.at[p, n])
            copy.start()
            departures.append(copy)
    for copy in departures:
        copy.wait()


def unpack_kernel(
    in_ref, o_hbm, dq_hbm, dk_hbm, dv_hbm, o_ref, dq_ref, dk_ref, dv_ref, sems
):
    x_hi = lax.axis_index("x_hi")
    copies = []
    for pair in range(HEADS // 2):
        columns = slice(pair * WIDTH, (pair + 1) * WIDTH)
        even, odd = 2 * pair, 2 * pair + 1
        kv0, kv1 = in_ref[slot_of(even, x_hi)], in_ref[slot_of(odd, x_hi)]
        qo0, qo1 = in_ref[slot_of(even, 1 - x_hi)], in_ref[slot_of(odd, 1 - x_hi)]
        dk_ref[:, columns] = turned_pair(kv0, kv1, 0)
        dv_ref[:, columns] = turned_pair(kv0, kv1, 1)
        dq_ref[:, columns] = lane_pair(qo0, qo1, 0)
        o_ref[:, columns] = lane_pair(qo0, qo1, 1)
        if (pair + 1) * WIDTH % PART == 0:
            p = pair * WIDTH // PART
            part = slice(p * PART, (p + 1) * PART)
            for n, (source, target) in enumerate(
                ((o_ref, o_hbm), (dq_ref, dq_hbm), (dk_ref, dk_hbm), (dv_ref, dv_hbm))
            ):
                copy = pltpu.make_async_copy(source.at[:, part], target.at[:, part], sems.at[p, n])
                copy.start()
                copies.append(copy)
    for copy in copies:
        copy.wait()


def split_kernel(in_ref, kv_ref, qg_ref, near_ref, far_ref):
    core = lax.axis_index("core")
    kv_at = core * HALF
    kv_ref[...] = in_ref[pl.ds(kv_at, HALF)]
    qg_ref[...] = in_ref[pl.ds((1 - core) * HALF, HALF)]
    near_ref[...] = in_ref[pl.ds(kv_at + core * QUARTER, QUARTER)]
    far_ref[...] = in_ref[pl.ds(kv_at + (1 - core) * QUARTER, QUARTER)]


def copy_kernel(in_ref, out_ref):
    out_ref[...] = in_ref[...]


def near_kernel(list_hbm, qg_ref, own_ref, mate_ref, near_ref, qo_ref, sums, *scratch):
    sums[...] = jnp.zeros_like(sums)
    core = lax.axis_index("core")
    attend(core, list_hbm, qg_ref, own_ref, mate_ref, (near_ref,), qo_ref, sums, *scratch)


def far_kernel(
    list_hbm, qg_ref, own_ref, mate_ref, near_ref, far_ref, sums_ref,
    qo_ref, own_out, mate_out, halo_out, sums, *scratch,
):
    sums[...] = sums_ref[...]
    core = lax.axis_index("core")
    attend(
        1 - core, list_hbm, qg_ref, own_ref, mate_ref, (near_ref, far_ref), qo_ref, sums, *scratch
    )
    own_at = 2 * core * HALF
    halo_out[...] = sums[pl.ds(2 * HALF - own_at, HALF)].astype(jnp.bfloat16)
    mate_out[...] = sums[HALF : 2 * HALF].astype(jnp.bfloat16)
    own_out[...] = sums[pl.ds(own_at, HALF)]


def attend(
    group, list_hbm, qg_ref, own_ref, mate_ref, halo_refs, qo_ref, accum,
    window, both_even, both_odd, pair_even, pair_odd, listed, table, sem,
):
    core, z = lax.axis_index("core"), lax.axis_index("z")
    own_at = 2 * core * HALF
    halo_at = 2 * HALF - own_at
    first = group * QUARTER
    first_query = z * PLANE + (1 - core) * HALF + first
    first_key = z * PLANE - core * HALF
    lanes = listed.shape[1]
    at = lax.div(first_query, lanes) * lanes
    copy = pltpu.make_async_copy(
        list_hbm.at[:, pl.ds(pl.multiple_of(at, lanes), lanes)], listed, sem
    )
    copy.start()
    window[pl.ds(own_at, HALF)] = own_ref[...]
    window[HALF : 2 * HALF] = mate_ref[...]
    for side, halo_ref in zip((core, 1 - core), halo_refs):
        window[pl.ds(halo_at + side * QUARTER, QUARTER)] = halo_ref[...]
    pair_odd[...] = jnp.zeros_like(pair_odd)
    copy.wait()

    def note(i, carry):
        for s in range(SLOTS):
            block = listed[s, first_query - at + i]
            dead = (block == first_query + i) if s else False
            table[i, s] = jnp.where(dead, -1, block - first_key)
        return carry

    lax.fori_loop(0, QUARTER, note, 0)

    def blocks_of(i):
        return [
            jnp.where(table[i, s] < 0, table[i, 0], table[i, s]) if s else table[i, 0]
            for s in range(SLOTS)
        ]

    left = lax.broadcasted_iota(jnp.int32, (BLOCK, WIDTH), 1) < HEAD_SIZE

    def query_rows(i):
        qg = qg_ref[first + i]
        zero = jnp.zeros_like(qg)
        return jnp.concatenate(
            [jnp.where(left, qg * jnp.bfloat16(SCALING), zero), jnp.where(left, zero, qg)], axis=0
        )

    top = lax.broadcasted_iota(jnp.int32, (WIDTH, BLOCK), 0) < HEAD_SIZE

    def query_columns(i):
        columns = qg_ref[first + i].T
        zero = jnp.zeros_like(columns)
        return jnp.concatenate(
            [jnp.where(top, columns * jnp.bfloat16(SCALING), zero), jnp.where(top, zero, columns)],
            axis=1,
        )

    def products(i, both):
        rows, blocks = query_rows(i), blocks_of(i)
        for k in range(PIECES):
            kv = jnp.concatenate([window[b] for b in blocks[k * PAIR : (k + 1) * PAIR]], axis=0)
            both[:, k * SPAN : (k + 1) * SPAN] = lax.dot_general(
                rows, kv, (((1,), (1,)), ((), ())), preferred_element_type=jnp.float32
            )
            yield

    def weigh(i, both, pair):
        live = [table[i, s] >= 0 for s in range(SLOTS)]
        for r in range(0, BLOCK, CHUNK):
            scores = jnp.concatenate(
                [
                    jnp.where(live[s], both[r : r + CHUNK, s * BLOCK : (s + 1) * BLOCK], -jnp.inf)
                    for s in range(SLOTS)
                ],
                axis=1,
            )
            dprob = both[BLOCK + r : BLOCK + r + CHUNK]
            weights = jnp.exp(scores - jnp.max(scores, axis=1, keepdims=True))
            probs = weights * (1.0 / jnp.sum(weights, axis=1, keepdims=True))
            terms = probs * dprob
            dscore = terms - probs * jnp.sum(terms, axis=1, keepdims=True)
            pair[r : r + CHUNK] = dscore.astype(jnp.bfloat16)
            pair[BLOCK + r : BLOCK + r + CHUNK] = probs.astype(jnp.bfloat16)
            if (r // CHUNK + 1) % (BLOCK // CHUNK // PIECES) == 0:
                yield

    def results(i, pair):
        blocks = blocks_of(i)
        columns = query_columns(i)
        mixed = None
        for k in range(PIECES):
            stacked = pair[:, k * SPAN : (k + 1) * SPAN]
            here = blocks[k * PAIR : (k + 1) * PAIR]
            kv = jnp.concatenate([window[b] for b in here], axis=0)
            part = jnp.dot(stacked, kv, preferred_element_type=jnp.float32)
            mixed = part if mixed is None else mixed + part
            grads = jnp.dot(columns, stacked, preferred_element_type=jnp.float32)
            for s, block in enumerate(here):
                accum[block] += grads[:, s * BLOCK : (s + 1) * BLOCK]
            if k == PIECES - 1:
                qo_ref[i] = jnp.where(left, mixed[:BLOCK] * SCALING, mixed[BLOCK:]).astype(
                    jnp.bfloat16
                )
            yield

    def beside(*stages):
        for _ in zip(*stages):
            pass

    beside(products(0, both_even))

    def step(j, carry):
        even, odd = 2 * j, 2 * j + 1
        beside(
            products(odd, both_odd),
            weigh(even, both_even, pair_even),
            results(jnp.maximum(even - 1, 0), pair_odd),
        )
        beside(
            products(jnp.minimum(even + 2, QUARTER - 1), both_even),
            weigh(odd, both_odd, pair_odd),
            results(even, pair_even),
        )
        return carry

    lax.fori_loop(0, QUARTER // 2, step, 0)
    beside(results(QUARTER - 1, pair_odd))


def halo_sum_kernel(own_ref, halo_ref, out_ref):
    out_ref[...] = own_ref[...] + halo_ref[...].astype(jnp.float32)


def sum_kernel(near_ref, far_ref, own_ref, mate_ref, out_ref):
    core = lax.axis_index("core")
    total = own_ref[...] + mate_ref[...].astype(jnp.float32)
    out_ref[pl.ds(core * HALF, HALF)] = total.astype(jnp.bfloat16)
    query_at = (1 - core) * HALF
    out_ref[pl.ds(query_at + core * QUARTER, QUARTER)] = near_ref[...]
    out_ref[pl.ds(query_at + (1 - core) * QUARTER, QUARTER)] = far_ref[...]


VMEM = pl.BlockSpec(memory_space=pltpu.VMEM)
ANY = pl.BlockSpec(memory_space=pl.ANY)
PARAMS = pltpu.CompilerParams(vmem_limit_bytes=VMEM_LIMIT)
EDGE_PARAMS = pltpu.CompilerParams(vmem_limit_bytes=60 * 1024 * 1024)


def moved(value, axes, target):
    sizes = [lax.axis_size(a) for a in axes]
    pairs = []
    for source in range(int(np.prod(sizes))):
        spot = [int(t) for t in np.unravel_index(source, sizes)]
        goal = target(*spot)
        if all(0 <= g < size for g, size in zip(goal, sizes)):
            pairs.append((source, int(np.ravel_multi_index(goal, sizes))))
    return lax.ppermute(value, axes, pairs)


def to_mate(value):
    return moved(value, ("core",), lambda c: (1 - c,))


def per_device(queries, key_rows, value_rows, cotangent, block_list):
    plane = jax.ShapeDtypeStruct((PLANE, BLOCK, WIDTH), jnp.bfloat16)
    packed = pl.pallas_call(
        pack_kernel,
        out_shape=plane,
        in_specs=[ANY] * 4,
        out_specs=ANY,
        scratch_shapes=[pltpu.VMEM(queries.shape, jnp.bfloat16)] * 4
        + [
            pltpu.VMEM(plane.shape, jnp.bfloat16),
            pltpu.SemaphoreType.DMA((PARTS, 4)),
            pltpu.SemaphoreType.DMA((PARTS, 2)),
        ],
        compiler_params=EDGE_PARAMS,
        name="pack",
    )(queries, key_rows, value_rows, cotangent)
    received = lax.all_to_all(packed, AXES, 0, 0, tiled=True)
    half = (HALF, BLOCK, WIDTH)
    quarter = (QUARTER, BLOCK, WIDTH)
    sums = (3 * HALF, BLOCK, WIDTH)
    key_value, query_grad_rows, near_part, far_part = pl.pallas_call(
        split_kernel,
        out_shape=[jax.ShapeDtypeStruct(half, jnp.bfloat16)] * 2
        + [jax.ShapeDtypeStruct(quarter, jnp.bfloat16)] * 2,
        in_specs=[VMEM],
        out_specs=[VMEM] * 4,
        compiler_params=PARAMS,
        name="split",
    )(received)

    def inward(value):
        return moved(value, ("z", "core"), lambda z, c: (z + (1 if c else -1), c))

    near = pl.pallas_call(
        copy_kernel,
        out_shape=jax.ShapeDtypeStruct(quarter, jnp.bfloat16),
        in_specs=[VMEM],
        out_specs=VMEM,
        compiler_params=PARAMS,
        cost_estimate=pl.CostEstimate(flops=1 << 32, bytes_accessed=1 << 20, transcendentals=0),
        name="near_copy",
    )(inward(near_part))
    mate = to_mate(key_value)
    far = inward(far_part)
    scratch = [
        pltpu.VMEM(sums, jnp.bfloat16),
        pltpu.VMEM((2 * BLOCK, KEYS), jnp.float32),
        pltpu.VMEM((2 * BLOCK, KEYS), jnp.float32),
        pltpu.VMEM((2 * BLOCK, KEYS), jnp.bfloat16),
        pltpu.VMEM((2 * BLOCK, KEYS), jnp.bfloat16),
        pltpu.SMEM((SLOTS, LANES), jnp.int32),
        pltpu.SMEM((QUARTER, SLOTS), jnp.int32),
        pltpu.SemaphoreType.DMA,
    ]
    work = pl.CostEstimate(
        flops=QUARTER * 6 * 2 * BLOCK * KEYS * WIDTH,
        bytes_accessed=1 << 20,
        transcendentals=QUARTER * BLOCK * KEYS,
    )
    query_near, near_sums = pl.pallas_call(
        near_kernel,
        out_shape=[
            jax.ShapeDtypeStruct(quarter, jnp.bfloat16),
            jax.ShapeDtypeStruct(sums, jnp.float32),
        ],
        in_specs=[ANY] + [VMEM] * 4,
        out_specs=[VMEM] * 2,
        scratch_shapes=scratch,
        compiler_params=PARAMS,
        cost_estimate=work,
        name="near",
    )(block_list.T, query_grad_rows, key_value, mate, near)
    query_far, own_part, mate_part, halo_part = pl.pallas_call(
        far_kernel,
        out_shape=[
            jax.ShapeDtypeStruct(quarter, jnp.bfloat16),
            jax.ShapeDtypeStruct(half, jnp.float32),
            jax.ShapeDtypeStruct(half, jnp.bfloat16),
            jax.ShapeDtypeStruct(half, jnp.bfloat16),
        ],
        in_specs=[ANY] + [VMEM] * 6,
        out_specs=[VMEM] * 4,
        scratch_shapes=[pltpu.VMEM(sums, jnp.float32)] + scratch,
        compiler_params=PARAMS,
        cost_estimate=work,
        name="far",
    )(block_list.T, query_grad_rows, key_value, mate, near, far, near_sums)
    mate_sum = to_mate(mate_part)
    halo_sum = moved(halo_part, ("z", "core"), lambda z, c: (z + (-1 if c else 1), c))
    own_sum = pl.pallas_call(
        halo_sum_kernel,
        out_shape=jax.ShapeDtypeStruct(half, jnp.float32),
        in_specs=[VMEM] * 2,
        out_specs=VMEM,
        compiler_params=PARAMS,
        name="halo_total",
    )(own_part, halo_sum)
    outgoing = pl.pallas_call(
        sum_kernel,
        out_shape=plane,
        in_specs=[VMEM] * 4,
        out_specs=VMEM,
        compiler_params=PARAMS,
        name="total",
    )(query_near, query_far, own_sum, mate_sum)
    returned = lax.all_to_all(outgoing, AXES, 0, 0, tiled=True)
    rows = jax.ShapeDtypeStruct(queries.shape, jnp.bfloat16)
    return pl.pallas_call(
        unpack_kernel,
        out_shape=[rows] * 4,
        in_specs=[VMEM],
        out_specs=[ANY] * 4,
        scratch_shapes=[pltpu.VMEM(queries.shape, jnp.bfloat16)] * 4
        + [pltpu.SemaphoreType.DMA((PARTS, 4))],
        compiler_params=PARAMS,
        name="unpack",
    )(returned)


def solution(mesh):
    fine = Mesh(mesh.devices.reshape(2, 4, 16, 2, 2), ("x_lo", "y", "z", "x_hi", "core"))
    rows = P(("z", "x_hi", "core", "x_lo", "y"), None)
    return jax.shard_map(
        per_device,
        mesh=fine,
        in_specs=(rows,) * 4 + (P(),),
        out_specs=(rows,) * 4,
        check_vma=False,
    )
```

```python
import jax
import jax.numpy as jnp
import numpy as np
from jax import lax
from jax.experimental import pallas as pl
from jax.experimental.pallas import tpu as pltpu
from jax.sharding import Mesh, PartitionSpec as P

HEADS = 16
HEAD_SIZE = 64
BLOCK = 128
WIDTH = 2 * HEAD_SIZE
SCALING = HEAD_SIZE ** (-0.5)
PLANE = 32
HALF = PLANE // 2
QUARTER = HALF // 2
SLOTS = 8
AXES = ("x_hi", "core", "x_lo", "y")
VMEM_LIMIT = 40 * 1024 * 1024
KEYS = SLOTS * BLOCK
CHUNK = 16
PIECES = 4
SPAN = KEYS // PIECES
PAIR = SLOTS // PIECES
LANES = 128
PART = 256
PARTS = HEADS * HEAD_SIZE // PART


def lane_pair(left, right, odd):
    start = HEAD_SIZE if odd else 0
    return jnp.concatenate(
        [left[:, start : start + HEAD_SIZE], right[:, start : start + HEAD_SIZE]], axis=1
    )


def turned_pair(left, right, odd):
    start = HEAD_SIZE if odd else 0
    return jnp.concatenate(
        [left[start : start + HEAD_SIZE], right[start : start + HEAD_SIZE]], axis=0
    ).T


def slot_of(head, core):
    return (head // 8) * 16 + core * 8 + head % 8


def pack_kernel(
    q_hbm, k_hbm, v_hbm, g_hbm, out_hbm, q_ref, k_ref, v_ref, g_ref, out_ref, in_sems, out_sems
):
    x_hi = lax.axis_index("x_hi")
    parts = [slice(p * PART, (p + 1) * PART) for p in range(PARTS)]
    arrivals = [
        [
            pltpu.make_async_copy(source.at[:, part], target.at[:, part], in_sems.at[p, n])
            for n, (source, target) in enumerate(
                ((k_hbm, k_ref), (v_hbm, v_ref), (q_hbm, q_ref), (g_hbm, g_ref))
            )
        ]
        for p, part in enumerate(parts)
    ]
    for group in arrivals:
        for copy in group:
            copy.start()
    departures = []
    for p in range(PARTS):
        for copy in arrivals[p]:
            copy.wait()
        heads = PART // HEAD_SIZE
        for head in range(p * heads, (p + 1) * heads):
            columns = slice(head // 2 * WIDTH, (head // 2 + 1) * WIDTH)
            out_ref[slot_of(head, x_hi)] = lane_pair(
                k_ref[:, columns], v_ref[:, columns], head % 2
            )
            out_ref[slot_of(head, 1 - x_hi)] = lane_pair(
                q_ref[:, columns], g_ref[:, columns], head % 2
            )
        for n in range(2):
            slots = pl.ds(slot_of(p * heads, n), heads)
            copy = pltpu.make_async_copy(out_ref.at[slots], out_hbm.at[slots], out_sems.at[p, n])
            copy.start()
            departures.append(copy)
    for copy in departures:
        copy.wait()


def unpack_kernel(
    in_ref, o_hbm, dq_hbm, dk_hbm, dv_hbm, o_ref, dq_ref, dk_ref, dv_ref, sems
):
    x_hi = lax.axis_index("x_hi")
    copies = []
    for pair in range(HEADS // 2):
        columns = slice(pair * WIDTH, (pair + 1) * WIDTH)
        even, odd = 2 * pair, 2 * pair + 1
        kv0, kv1 = in_ref[slot_of(even, x_hi)], in_ref[slot_of(odd, x_hi)]
        qo0, qo1 = in_ref[slot_of(even, 1 - x_hi)], in_ref[slot_of(odd, 1 - x_hi)]
        dk_ref[:, columns] = turned_pair(kv0, kv1, 0)
        dv_ref[:, columns] = turned_pair(kv0, kv1, 1)
        dq_ref[:, columns] = lane_pair(qo0, qo1, 0)
        o_ref[:, columns] = lane_pair(qo0, qo1, 1)
        if (pair + 1) * WIDTH % PART == 0:
            p = pair * WIDTH // PART
            part = slice(p * PART, (p + 1) * PART)
            for n, (source, target) in enumerate(
                ((o_ref, o_hbm), (dq_ref, dq_hbm), (dk_ref, dk_hbm), (dv_ref, dv_hbm))
            ):
                copy = pltpu.make_async_copy(source.at[:, part], target.at[:, part], sems.at[p, n])
                copy.start()
                copies.append(copy)
    for copy in copies:
        copy.wait()


def split_kernel(in_ref, kv_ref, qg_ref, near_ref, far_ref):
    core = lax.axis_index("core")
    kv_at = core * HALF
    kv_ref[...] = in_ref[pl.ds(kv_at, HALF)]
    qg_ref[...] = in_ref[pl.ds((1 - core) * HALF, HALF)]
    near_ref[...] = in_ref[pl.ds(kv_at + core * QUARTER, QUARTER)]
    far_ref[...] = in_ref[pl.ds(kv_at + (1 - core) * QUARTER, QUARTER)]


def copy_kernel(in_ref, out_ref):
    out_ref[...] = in_ref[...]


def near_kernel(list_hbm, qg_ref, own_ref, mate_ref, near_ref, qo_ref, sums, *scratch):
    sums[...] = jnp.zeros_like(sums)
    core = lax.axis_index("core")
    attend(core, list_hbm, qg_ref, own_ref, mate_ref, (near_ref,), qo_ref, sums, *scratch)


def far_kernel(
    list_hbm, qg_ref, own_ref, mate_ref, near_ref, far_ref, sums_ref,
    qo_ref, own_out, mate_out, halo_out, sums, *scratch,
):
    sums[...] = sums_ref[...]
    core = lax.axis_index("core")
    attend(
        1 - core, list_hbm, qg_ref, own_ref, mate_ref, (near_ref, far_ref), qo_ref, sums, *scratch
    )
    own_at = 2 * core * HALF
    halo_out[...] = sums[pl.ds(2 * HALF - own_at, HALF)].astype(jnp.bfloat16)
    mate_out[...] = sums[HALF : 2 * HALF].astype(jnp.bfloat16)
    own_out[...] = sums[pl.ds(own_at, HALF)]


def attend(
    group, list_hbm, qg_ref, own_ref, mate_ref, halo_refs, qo_ref, accum,
    window, both_even, both_odd, pair_even, pair_odd, listed, table, sem,
):
    core, z = lax.axis_index("core"), lax.axis_index("z")
    own_at = 2 * core * HALF
    halo_at = 2 * HALF - own_at
    first = group * QUARTER
    first_query = z * PLANE + (1 - core) * HALF + first
    first_key = z * PLANE - core * HALF
    lanes = listed.shape[1]
    at = lax.div(first_query, lanes) * lanes
    copy = pltpu.make_async_copy(
        list_hbm.at[:, pl.ds(pl.multiple_of(at, lanes), lanes)], listed, sem
    )
    copy.start()
    window[pl.ds(own_at, HALF)] = own_ref[...]
    window[HALF : 2 * HALF] = mate_ref[...]
    for side, halo_ref in zip((core, 1 - core), halo_refs):
        window[pl.ds(halo_at + side * QUARTER, QUARTER)] = halo_ref[...]
    copy.wait()

    def note(i, carry):
        for s in range(SLOTS):
            block = listed[s, first_query - at + i]
            dead = (block == first_query + i) if s else False
            table[i, s] = jnp.where(dead, -1, block - first_key)
        return carry

    lax.fori_loop(0, QUARTER, note, 0)

    def blocks_of(i):
        return [
            jnp.where(table[i, s] < 0, table[i, 0], table[i, s]) if s else table[i, 0]
            for s in range(SLOTS)
        ]

    left = lax.broadcasted_iota(jnp.int32, (BLOCK, WIDTH), 1) < HEAD_SIZE

    def query_rows(i):
        qg = qg_ref[first + i]
        zero = jnp.zeros_like(qg)
        return jnp.concatenate(
            [jnp.where(left, qg * jnp.bfloat16(SCALING), zero), jnp.where(left, zero, qg)], axis=0
        )

    top = lax.broadcasted_iota(jnp.int32, (WIDTH, BLOCK), 0) < HEAD_SIZE

    def query_columns(i):
        columns = qg_ref[first + i].T
        zero = jnp.zeros_like(columns)
        return jnp.concatenate(
            [jnp.where(top, columns * jnp.bfloat16(SCALING), zero), jnp.where(top, zero, columns)],
            axis=1,
        )

    def products(i, both):
        rows, blocks = query_rows(i), blocks_of(i)
        for k in range(PIECES):
            kv = jnp.concatenate([window[b] for b in blocks[k * PAIR : (k + 1) * PAIR]], axis=0)
            both[:, k * SPAN : (k + 1) * SPAN] = lax.dot_general(
                rows, kv, (((1,), (1,)), ((), ())), preferred_element_type=jnp.float32
            )
            yield

    def weigh(i, both, pair):
        live = [table[i, s] >= 0 for s in range(SLOTS)]
        for r in range(0, BLOCK, CHUNK):
            scores = jnp.concatenate(
                [
                    jnp.where(live[s], both[r : r + CHUNK, s * BLOCK : (s + 1) * BLOCK], -jnp.inf)
                    for s in range(SLOTS)
                ],
                axis=1,
            )
            dprob = both[BLOCK + r : BLOCK + r + CHUNK]
            weights = jnp.exp(scores - jnp.max(scores, axis=1, keepdims=True))
            probs = weights * (1.0 / jnp.sum(weights, axis=1, keepdims=True))
            terms = probs * dprob
            dscore = terms - probs * jnp.sum(terms, axis=1, keepdims=True)
            pair[r : r + CHUNK] = dscore.astype(jnp.bfloat16)
            pair[BLOCK + r : BLOCK + r + CHUNK] = probs.astype(jnp.bfloat16)
            if (r // CHUNK + 1) % (BLOCK // CHUNK // PIECES) == 0:
                yield

    def results(i, pair):
        blocks = blocks_of(i)
        columns = query_columns(i)
        mixed = None
        for k in range(PIECES):
            stacked = pair[:, k * SPAN : (k + 1) * SPAN]
            here = blocks[k * PAIR : (k + 1) * PAIR]
            kv = jnp.concatenate([window[b] for b in here], axis=0)
            part = jnp.dot(stacked, kv, preferred_element_type=jnp.float32)
            mixed = part if mixed is None else mixed + part
            grads = jnp.dot(columns, stacked, preferred_element_type=jnp.float32)
            for s, block in enumerate(here):
                accum[block] += grads[:, s * BLOCK : (s + 1) * BLOCK]
            if k == PIECES - 1:
                qo_ref[i] = jnp.where(left, mixed[:BLOCK] * SCALING, mixed[BLOCK:]).astype(
                    jnp.bfloat16
                )
            yield

    both, pair = (both_even, both_odd), (pair_even, pair_odd)
    for i in range(-1, QUARTER + 1):
        stages = []
        if i + 1 < QUARTER:
            stages.append(products(i + 1, both[(i + 1) % 2]))
        if 0 <= i < QUARTER:
            stages.append(weigh(i, both[i % 2], pair[i % 2]))
        if i > 0:
            stages.append(results(i - 1, pair[(i - 1) % 2]))
        for _ in zip(*stages):
            pass


def halo_sum_kernel(own_ref, halo_ref, out_ref):
    out_ref[...] = own_ref[...] + halo_ref[...].astype(jnp.float32)


def sum_kernel(near_ref, far_ref, own_ref, mate_ref, out_ref):
    core = lax.axis_index("core")
    total = own_ref[...] + mate_ref[...].astype(jnp.float32)
    out_ref[pl.ds(core * HALF, HALF)] = total.astype(jnp.bfloat16)
    query_at = (1 - core) * HALF
    out_ref[pl.ds(query_at + core * QUARTER, QUARTER)] = near_ref[...]
    out_ref[pl.ds(query_at + (1 - core) * QUARTER, QUARTER)] = far_ref[...]


VMEM = pl.BlockSpec(memory_space=pltpu.VMEM)
ANY = pl.BlockSpec(memory_space=pl.ANY)
PARAMS = pltpu.CompilerParams(vmem_limit_bytes=VMEM_LIMIT)
EDGE_PARAMS = pltpu.CompilerParams(vmem_limit_bytes=60 * 1024 * 1024)


def moved(value, axes, target):
    sizes = [lax.axis_size(a) for a in axes]
    pairs = []
    for source in range(int(np.prod(sizes))):
        spot = [int(t) for t in np.unravel_index(source, sizes)]
        goal = target(*spot)
        if all(0 <= g < size for g, size in zip(goal, sizes)):
            pairs.append((source, int(np.ravel_multi_index(goal, sizes))))
    return lax.ppermute(value, axes, pairs)


def to_mate(value):
    return moved(value, ("core",), lambda c: (1 - c,))


def per_device(queries, key_rows, value_rows, cotangent, block_list):
    plane = jax.ShapeDtypeStruct((PLANE, BLOCK, WIDTH), jnp.bfloat16)
    packed = pl.pallas_call(
        pack_kernel,
        out_shape=plane,
        in_specs=[ANY] * 4,
        out_specs=ANY,
        scratch_shapes=[pltpu.VMEM(queries.shape, jnp.bfloat16)] * 4
        + [
            pltpu.VMEM(plane.shape, jnp.bfloat16),
            pltpu.SemaphoreType.DMA((PARTS, 4)),
            pltpu.SemaphoreType.DMA((PARTS, 2)),
        ],
        compiler_params=EDGE_PARAMS,
        name="pack",
    )(queries, key_rows, value_rows, cotangent)
    received = lax.all_to_all(packed, AXES, 0, 0, tiled=True)
    half = (HALF, BLOCK, WIDTH)
    quarter = (QUARTER, BLOCK, WIDTH)
    sums = (3 * HALF, BLOCK, WIDTH)
    key_value, query_grad_rows, near_part, far_part = pl.pallas_call(
        split_kernel,
        out_shape=[jax.ShapeDtypeStruct(half, jnp.bfloat16)] * 2
        + [jax.ShapeDtypeStruct(quarter, jnp.bfloat16)] * 2,
        in_specs=[VMEM],
        out_specs=[VMEM] * 4,
        compiler_params=PARAMS,
        name="split",
    )(received)

    def inward(value):
        return moved(value, ("z", "core"), lambda z, c: (z + (1 if c else -1), c))

    near = pl.pallas_call(
        copy_kernel,
        out_shape=jax.ShapeDtypeStruct(quarter, jnp.bfloat16),
        in_specs=[VMEM],
        out_specs=VMEM,
        compiler_params=PARAMS,
        cost_estimate=pl.CostEstimate(flops=1 << 32, bytes_accessed=1 << 20, transcendentals=0),
        name="near_copy",
    )(inward(near_part))
    mate = to_mate(key_value)
    far = inward(far_part)
    scratch = [
        pltpu.VMEM(sums, jnp.bfloat16),
        pltpu.VMEM((2 * BLOCK, KEYS), jnp.float32),
        pltpu.VMEM((2 * BLOCK, KEYS), jnp.float32),
        pltpu.VMEM((2 * BLOCK, KEYS), jnp.bfloat16),
        pltpu.VMEM((2 * BLOCK, KEYS), jnp.bfloat16),
        pltpu.SMEM((SLOTS, LANES), jnp.int32),
        pltpu.SMEM((QUARTER, SLOTS), jnp.int32),
        pltpu.SemaphoreType.DMA,
    ]
    work = pl.CostEstimate(
        flops=QUARTER * 6 * 2 * BLOCK * KEYS * WIDTH,
        bytes_accessed=1 << 20,
        transcendentals=QUARTER * BLOCK * KEYS,
    )
    query_near, near_sums = pl.pallas_call(
        near_kernel,
        out_shape=[
            jax.ShapeDtypeStruct(quarter, jnp.bfloat16),
            jax.ShapeDtypeStruct(sums, jnp.float32),
        ],
        in_specs=[ANY] + [VMEM] * 4,
        out_specs=[VMEM] * 2,
        scratch_shapes=scratch,
        compiler_params=PARAMS,
        cost_estimate=work,
        name="near",
    )(block_list.T, query_grad_rows, key_value, mate, near)
    query_far, own_part, mate_part, halo_part = pl.pallas_call(
        far_kernel,
        out_shape=[
            jax.ShapeDtypeStruct(quarter, jnp.bfloat16),
            jax.ShapeDtypeStruct(half, jnp.float32),
            jax.ShapeDtypeStruct(half, jnp.bfloat16),
            jax.ShapeDtypeStruct(half, jnp.bfloat16),
        ],
        in_specs=[ANY] + [VMEM] * 6,
        out_specs=[VMEM] * 4,
        scratch_shapes=[pltpu.VMEM(sums, jnp.float32)] + scratch,
        compiler_params=PARAMS,
        cost_estimate=work,
        name="far",
    )(block_list.T, query_grad_rows, key_value, mate, near, far, near_sums)
    mate_sum = to_mate(mate_part)
    halo_sum = moved(halo_part, ("z", "core"), lambda z, c: (z + (-1 if c else 1), c))
    own_sum = pl.pallas_call(
        halo_sum_kernel,
        out_shape=jax.ShapeDtypeStruct(half, jnp.float32),
        in_specs=[VMEM] * 2,
        out_specs=VMEM,
        compiler_params=PARAMS,
        name="halo_total",
    )(own_part, halo_sum)
    outgoing = pl.pallas_call(
        sum_kernel,
        out_shape=plane,
        in_specs=[VMEM] * 4,
        out_specs=VMEM,
        compiler_params=PARAMS,
        name="total",
    )(query_near, query_far, own_sum, mate_sum)
    returned = lax.all_to_all(outgoing, AXES, 0, 0, tiled=True)
    rows = jax.ShapeDtypeStruct(queries.shape, jnp.bfloat16)
    return pl.pallas_call(
        unpack_kernel,
        out_shape=[rows] * 4,
        in_specs=[VMEM],
        out_specs=[ANY] * 4,
        scratch_shapes=[pltpu.VMEM(queries.shape, jnp.bfloat16)] * 4
        + [pltpu.SemaphoreType.DMA((PARTS, 4))],
        compiler_params=PARAMS,
        name="unpack",
    )(returned)


def solution(mesh):
    fine = Mesh(mesh.devices.reshape(2, 4, 16, 2, 2), ("x_lo", "y", "z", "x_hi", "core"))
    rows = P(("z", "x_hi", "core", "x_lo", "y"), None)
    return jax.shard_map(
        per_device,
        mesh=fine,
        in_specs=(rows,) * 4 + (P(),),
        out_specs=(rows,) * 4,
        check_vma=False,
    )
```

```python
import jax
import jax.numpy as jnp
import numpy as np
from jax import lax
from jax.experimental import pallas as pl
from jax.experimental.pallas import tpu as pltpu
from jax.sharding import Mesh, PartitionSpec as P

HEADS = 16
HEAD_SIZE = 64
BLOCK = 128
WIDTH = 2 * HEAD_SIZE
SCALING = HEAD_SIZE ** (-0.5)
PLANE = 32
HALF = PLANE // 2
QUARTER = HALF // 2
SLOTS = 8
AXES = ("x_hi", "core", "x_lo", "y")
VMEM_LIMIT = 40 * 1024 * 1024
KEYS = SLOTS * BLOCK
CHUNK = 16
PIECES = 4
SPAN = KEYS // PIECES
PAIR = SLOTS // PIECES
LANES = 128
PART = 256
PARTS = HEADS * HEAD_SIZE // PART


def lane_pair(left, right, odd):
    start = HEAD_SIZE if odd else 0
    return jnp.concatenate(
        [left[:, start : start + HEAD_SIZE], right[:, start : start + HEAD_SIZE]], axis=1
    )


def turned_pair(left, right, odd):
    start = HEAD_SIZE if odd else 0
    return jnp.concatenate(
        [left[start : start + HEAD_SIZE], right[start : start + HEAD_SIZE]], axis=0
    ).T


def slot_of(head, core):
    return (head // 8) * 16 + core * 8 + head % 8


def pack_kernel(
    q_hbm, k_hbm, v_hbm, g_hbm, out_hbm, q_ref, k_ref, v_ref, g_ref, out_ref, in_sems, out_sems
):
    x_hi = lax.axis_index("x_hi")
    parts = [slice(p * PART, (p + 1) * PART) for p in range(PARTS)]
    arrivals = [
        [
            pltpu.make_async_copy(source.at[:, part], target.at[:, part], in_sems.at[p, n])
            for n, (source, target) in enumerate(
                ((k_hbm, k_ref), (v_hbm, v_ref), (q_hbm, q_ref), (g_hbm, g_ref))
            )
        ]
        for p, part in enumerate(parts)
    ]
    for group in arrivals:
        for copy in group:
            copy.start()
    departures = []
    for p in range(PARTS):
        for copy in arrivals[p]:
            copy.wait()
        heads = PART // HEAD_SIZE
        for head in range(p * heads, (p + 1) * heads):
            columns = slice(head // 2 * WIDTH, (head // 2 + 1) * WIDTH)
            out_ref[slot_of(head, x_hi)] = lane_pair(
                k_ref[:, columns], v_ref[:, columns], head % 2
            )
            out_ref[slot_of(head, 1 - x_hi)] = lane_pair(
                q_ref[:, columns], g_ref[:, columns], head % 2
            )
        for n in range(2):
            slots = pl.ds(slot_of(p * heads, n), heads)
            copy = pltpu.make_async_copy(out_ref.at[slots], out_hbm.at[slots], out_sems.at[p, n])
            copy.start()
            departures.append(copy)
    for copy in departures:
        copy.wait()


def unpack_kernel(
    in_ref, o_hbm, dq_hbm, dk_hbm, dv_hbm, o_ref, dq_ref, dk_ref, dv_ref, sems
):
    x_hi = lax.axis_index("x_hi")
    copies = []
    for n, (ref, hbm, core, odd, joined) in enumerate(
        (
            (dk_ref, dk_hbm, x_hi, 0, turned_pair),
            (dv_ref, dv_hbm, x_hi, 1, turned_pair),
            (dq_ref, dq_hbm, 1 - x_hi, 0, lane_pair),
            (o_ref, o_hbm, 1 - x_hi, 1, lane_pair),
        )
    ):
        for pair in range(HEADS // 2):
            columns = slice(pair * WIDTH, (pair + 1) * WIDTH)
            ref[:, columns] = joined(
                in_ref[slot_of(2 * pair, core)], in_ref[slot_of(2 * pair + 1, core)], odd
            )
        copy = pltpu.make_async_copy(ref, hbm, sems.at[n])
        copy.start()
        copies.append(copy)
    for copy in copies:
        copy.wait()


def split_kernel(in_ref, kv_ref, qg_ref, near_ref, far_ref):
    core = lax.axis_index("core")
    kv_at = core * HALF
    kv_ref[...] = in_ref[pl.ds(kv_at, HALF)]
    qg_ref[...] = in_ref[pl.ds((1 - core) * HALF, HALF)]
    near_ref[...] = in_ref[pl.ds(kv_at + core * QUARTER, QUARTER)]
    far_ref[...] = in_ref[pl.ds(kv_at + (1 - core) * QUARTER, QUARTER)]


def copy_kernel(in_ref, out_ref):
    out_ref[...] = in_ref[...]


def near_kernel(list_hbm, qg_ref, own_ref, mate_ref, near_ref, qo_ref, sums, *scratch):
    sums[...] = jnp.zeros_like(sums)
    core = lax.axis_index("core")
    attend(core, list_hbm, qg_ref, own_ref, mate_ref, (near_ref,), qo_ref, sums, *scratch)


def far_kernel(
    list_hbm, qg_ref, own_ref, mate_ref, near_ref, far_ref, sums_ref,
    qo_ref, own_out, mate_out, halo_out, sums, *scratch,
):
    sums[...] = sums_ref[...]
    core = lax.axis_index("core")
    attend(
        1 - core, list_hbm, qg_ref, own_ref, mate_ref, (near_ref, far_ref), qo_ref, sums, *scratch
    )
    own_at = 2 * core * HALF
    halo_out[...] = sums[pl.ds(2 * HALF - own_at, HALF)].astype(jnp.bfloat16)
    mate_out[...] = sums[HALF : 2 * HALF].astype(jnp.bfloat16)
    own_out[...] = sums[pl.ds(own_at, HALF)]


def attend(
    group, list_hbm, qg_ref, own_ref, mate_ref, halo_refs, qo_ref, accum,
    window, both_even, both_odd, pair_even, pair_odd, listed, table, sem,
):
    core, z = lax.axis_index("core"), lax.axis_index("z")
    own_at = 2 * core * HALF
    halo_at = 2 * HALF - own_at
    first = group * QUARTER
    first_query = z * PLANE + (1 - core) * HALF + first
    first_key = z * PLANE - core * HALF
    lanes = listed.shape[1]
    at = lax.div(first_query, lanes) * lanes
    copy = pltpu.make_async_copy(
        list_hbm.at[:, pl.ds(pl.multiple_of(at, lanes), lanes)], listed, sem
    )
    copy.start()
    window[pl.ds(own_at, HALF)] = own_ref[...]
    window[HALF : 2 * HALF] = mate_ref[...]
    for side, halo_ref in zip((core, 1 - core), halo_refs):
        window[pl.ds(halo_at + side * QUARTER, QUARTER)] = halo_ref[...]
    copy.wait()

    for i in range(QUARTER):
        for s in range(SLOTS):
            block = listed[s, first_query - at + i]
            dead = (block == first_query + i) if s else False
            table[i, s] = jnp.where(dead, -1, block - first_key)

    def blocks_of(i):
        return [
            jnp.where(table[i, s] < 0, table[i, 0], table[i, s]) if s else table[i, 0]
            for s in range(SLOTS)
        ]

    left = lax.broadcasted_iota(jnp.int32, (BLOCK, WIDTH), 1) < HEAD_SIZE

    def query_rows(i):
        qg = qg_ref[first + i]
        zero = jnp.zeros_like(qg)
        return jnp.concatenate(
            [jnp.where(left, qg * jnp.bfloat16(SCALING), zero), jnp.where(left, zero, qg)], axis=0
        )

    top = lax.broadcasted_iota(jnp.int32, (WIDTH, BLOCK), 0) < HEAD_SIZE

    def query_columns(i):
        columns = qg_ref[first + i].T
        zero = jnp.zeros_like(columns)
        return jnp.concatenate(
            [jnp.where(top, columns * jnp.bfloat16(SCALING), zero), jnp.where(top, zero, columns)],
            axis=1,
        )

    def products(i, both):
        rows, blocks = query_rows(i), blocks_of(i)
        for k in range(PIECES):
            kv = jnp.concatenate([window[b] for b in blocks[k * PAIR : (k + 1) * PAIR]], axis=0)
            both[:, k * SPAN : (k + 1) * SPAN] = lax.dot_general(
                rows, kv, (((1,), (1,)), ((), ())), preferred_element_type=jnp.float32
            )
            yield

    def weigh(i, both, pair):
        live = [table[i, s] >= 0 for s in range(SLOTS)]
        for r in range(0, BLOCK, CHUNK):
            scores = jnp.concatenate(
                [
                    jnp.where(live[s], both[r : r + CHUNK, s * BLOCK : (s + 1) * BLOCK], -jnp.inf)
                    for s in range(SLOTS)
                ],
                axis=1,
            )
            dprob = both[BLOCK + r : BLOCK + r + CHUNK]
            weights = jnp.exp(scores - jnp.max(scores, axis=1, keepdims=True))
            probs = weights * (1.0 / jnp.sum(weights, axis=1, keepdims=True))
            terms = probs * dprob
            dscore = terms - probs * jnp.sum(terms, axis=1, keepdims=True)
            pair[r : r + CHUNK] = dscore.astype(jnp.bfloat16)
            pair[BLOCK + r : BLOCK + r + CHUNK] = probs.astype(jnp.bfloat16)
            if (r // CHUNK + 1) % (BLOCK // CHUNK // PIECES) == 0:
                yield

    def results(i, pair):
        blocks = blocks_of(i)
        columns = query_columns(i)
        mixed = None
        for k in range(PIECES):
            stacked = pair[:, k * SPAN : (k + 1) * SPAN]
            here = blocks[k * PAIR : (k + 1) * PAIR]
            kv = jnp.concatenate([window[b] for b in here], axis=0)
            part = jnp.dot(stacked, kv, preferred_element_type=jnp.float32)
            mixed = part if mixed is None else mixed + part
            grads = jnp.dot(columns, stacked, preferred_element_type=jnp.float32)
            for s, block in enumerate(here):
                accum[block] += grads[:, s * BLOCK : (s + 1) * BLOCK]
            if k == PIECES - 1:
                qo_ref[i] = jnp.where(left, mixed[:BLOCK] * SCALING, mixed[BLOCK:]).astype(
                    jnp.bfloat16
                )
            yield

    both, pair = (both_even, both_odd), (pair_even, pair_odd)
    for i in range(-1, QUARTER + 1):
        stages = []
        if i + 1 < QUARTER:
            stages.append(products(i + 1, both[(i + 1) % 2]))
        if 0 <= i < QUARTER:
            stages.append(weigh(i, both[i % 2], pair[i % 2]))
        if i > 0:
            stages.append(results(i - 1, pair[(i - 1) % 2]))
        for _ in zip(*stages):
            pass


def halo_sum_kernel(own_ref, halo_ref, out_ref):
    out_ref[...] = own_ref[...] + halo_ref[...].astype(jnp.float32)


def sum_kernel(near_ref, far_ref, own_ref, mate_ref, out_ref):
    core = lax.axis_index("core")
    total = own_ref[...] + mate_ref[...].astype(jnp.float32)
    out_ref[pl.ds(core * HALF, HALF)] = total.astype(jnp.bfloat16)
    query_at = (1 - core) * HALF
    out_ref[pl.ds(query_at + core * QUARTER, QUARTER)] = near_ref[...]
    out_ref[pl.ds(query_at + (1 - core) * QUARTER, QUARTER)] = far_ref[...]


VMEM = pl.BlockSpec(memory_space=pltpu.VMEM)
ANY = pl.BlockSpec(memory_space=pl.ANY)
PARAMS = pltpu.CompilerParams(vmem_limit_bytes=VMEM_LIMIT)
EDGE_PARAMS = pltpu.CompilerParams(vmem_limit_bytes=60 * 1024 * 1024)


def moved(value, axes, target):
    sizes = [lax.axis_size(a) for a in axes]
    pairs = []
    for source in range(int(np.prod(sizes))):
        spot = [int(t) for t in np.unravel_index(source, sizes)]
        goal = target(*spot)
        if all(0 <= g < size for g, size in zip(goal, sizes)):
            pairs.append((source, int(np.ravel_multi_index(goal, sizes))))
    return lax.ppermute(value, axes, pairs)


def to_mate(value):
    return moved(value, ("core",), lambda c: (1 - c,))


def per_device(queries, key_rows, value_rows, cotangent, block_list):
    plane = jax.ShapeDtypeStruct((PLANE, BLOCK, WIDTH), jnp.bfloat16)
    packed = pl.pallas_call(
        pack_kernel,
        out_shape=plane,
        in_specs=[ANY] * 4,
        out_specs=ANY,
        scratch_shapes=[pltpu.VMEM(queries.shape, jnp.bfloat16)] * 4
        + [
            pltpu.VMEM(plane.shape, jnp.bfloat16),
            pltpu.SemaphoreType.DMA((PARTS, 4)),
            pltpu.SemaphoreType.DMA((PARTS, 2)),
        ],
        compiler_params=EDGE_PARAMS,
        name="pack",
    )(queries, key_rows, value_rows, cotangent)
    received = lax.all_to_all(packed, AXES, 0, 0, tiled=True)
    half = (HALF, BLOCK, WIDTH)
    quarter = (QUARTER, BLOCK, WIDTH)
    sums = (3 * HALF, BLOCK, WIDTH)
    key_value, query_grad_rows, near_part, far_part = pl.pallas_call(
        split_kernel,
        out_shape=[jax.ShapeDtypeStruct(half, jnp.bfloat16)] * 2
        + [jax.ShapeDtypeStruct(quarter, jnp.bfloat16)] * 2,
        in_specs=[VMEM],
        out_specs=[VMEM] * 4,
        compiler_params=PARAMS,
        name="split",
    )(received)

    def inward(value):
        return moved(value, ("z", "core"), lambda z, c: (z + (1 if c else -1), c))

    near = pl.pallas_call(
        copy_kernel,
        out_shape=jax.ShapeDtypeStruct(quarter, jnp.bfloat16),
        in_specs=[VMEM],
        out_specs=VMEM,
        compiler_params=PARAMS,
        cost_estimate=pl.CostEstimate(flops=1 << 32, bytes_accessed=1 << 20, transcendentals=0),
        name="near_copy",
    )(inward(near_part))
    mate = to_mate(key_value)
    far = inward(far_part)
    scratch = [
        pltpu.VMEM(sums, jnp.bfloat16),
        pltpu.VMEM((2 * BLOCK, KEYS), jnp.float32),
        pltpu.VMEM((2 * BLOCK, KEYS), jnp.float32),
        pltpu.VMEM((2 * BLOCK, KEYS), jnp.bfloat16),
        pltpu.VMEM((2 * BLOCK, KEYS), jnp.bfloat16),
        pltpu.SMEM((SLOTS, LANES), jnp.int32),
        pltpu.SMEM((QUARTER, SLOTS), jnp.int32),
        pltpu.SemaphoreType.DMA,
    ]
    work = pl.CostEstimate(
        flops=QUARTER * 6 * 2 * BLOCK * KEYS * WIDTH,
        bytes_accessed=1 << 20,
        transcendentals=QUARTER * BLOCK * KEYS,
    )
    query_near, near_sums = pl.pallas_call(
        near_kernel,
        out_shape=[
            jax.ShapeDtypeStruct(quarter, jnp.bfloat16),
            jax.ShapeDtypeStruct(sums, jnp.float32),
        ],
        in_specs=[ANY] + [VMEM] * 4,
        out_specs=[VMEM] * 2,
        scratch_shapes=scratch,
        compiler_params=PARAMS,
        cost_estimate=work,
        name="near",
    )(block_list.T, query_grad_rows, key_value, mate, near)
    query_far, own_part, mate_part, halo_part = pl.pallas_call(
        far_kernel,
        out_shape=[
            jax.ShapeDtypeStruct(quarter, jnp.bfloat16),
            jax.ShapeDtypeStruct(half, jnp.float32),
            jax.ShapeDtypeStruct(half, jnp.bfloat16),
            jax.ShapeDtypeStruct(half, jnp.bfloat16),
        ],
        in_specs=[ANY] + [VMEM] * 6,
        out_specs=[VMEM] * 4,
        scratch_shapes=[pltpu.VMEM(sums, jnp.float32)] + scratch,
        compiler_params=PARAMS,
        cost_estimate=work,
        name="far",
    )(block_list.T, query_grad_rows, key_value, mate, near, far, near_sums)
    mate_sum = to_mate(mate_part)
    halo_sum = moved(halo_part, ("z", "core"), lambda z, c: (z + (-1 if c else 1), c))
    own_sum = pl.pallas_call(
        halo_sum_kernel,
        out_shape=jax.ShapeDtypeStruct(half, jnp.float32),
        in_specs=[VMEM] * 2,
        out_specs=VMEM,
        compiler_params=PARAMS,
        name="halo_total",
    )(own_part, halo_sum)
    outgoing = pl.pallas_call(
        sum_kernel,
        out_shape=plane,
        in_specs=[VMEM] * 4,
        out_specs=VMEM,
        compiler_params=PARAMS,
        name="total",
    )(query_near, query_far, own_sum, mate_sum)
    returned = lax.all_to_all(outgoing, AXES, 0, 0, tiled=True)
    rows = jax.ShapeDtypeStruct(queries.shape, jnp.bfloat16)
    return pl.pallas_call(
        unpack_kernel,
        out_shape=[rows] * 4,
        in_specs=[VMEM],
        out_specs=[ANY] * 4,
        scratch_shapes=[pltpu.VMEM(queries.shape, jnp.bfloat16)] * 4
        + [pltpu.SemaphoreType.DMA((4,))],
        compiler_params=PARAMS,
        name="unpack",
    )(returned)


def solution(mesh):
    fine = Mesh(mesh.devices.reshape(2, 4, 16, 2, 2), ("x_lo", "y", "z", "x_hi", "core"))
    rows = P(("z", "x_hi", "core", "x_lo", "y"), None)
    return jax.shard_map(
        per_device,
        mesh=fine,
        in_specs=(rows,) * 4 + (P(),),
        out_specs=(rows,) * 4,
        check_vma=False,
    )
```

```python
import jax
import jax.numpy as jnp
import numpy as np
from jax import lax
from jax.experimental import pallas as pl
from jax.experimental.pallas import tpu as pltpu
from jax.sharding import Mesh, PartitionSpec as P

HEADS = 16
HEAD_SIZE = 64
BLOCK = 128
WIDTH = 2 * HEAD_SIZE
SCALING = HEAD_SIZE ** (-0.5)
PLANE = 32
HALF = PLANE // 2
QUARTER = HALF // 2
SLOTS = 8
AXES = ("x_hi", "core", "x_lo", "y")
VMEM_LIMIT = 40 * 1024 * 1024
KEYS = SLOTS * BLOCK
CHUNK = 16
PIECES = 4
SPAN = KEYS // PIECES
PAIR = SLOTS // PIECES
LANES = 128
PART = 256
PARTS = HEADS * HEAD_SIZE // PART


def lane_pair(left, right, odd):
    start = HEAD_SIZE if odd else 0
    return jnp.concatenate(
        [left[:, start : start + HEAD_SIZE], right[:, start : start + HEAD_SIZE]], axis=1
    )


def turned_pair(left, right, odd):
    start = HEAD_SIZE if odd else 0
    return jnp.concatenate(
        [left[start : start + HEAD_SIZE], right[start : start + HEAD_SIZE]], axis=0
    ).T


def slot_of(head, core):
    return (head // 8) * 16 + core * 8 + head % 8


def pack_kernel(
    q_hbm, k_hbm, v_hbm, g_hbm, out_hbm, q_ref, k_ref, v_ref, g_ref, out_ref, in_sems, out_sems
):
    x_hi = lax.axis_index("x_hi")
    parts = [slice(p * PART, (p + 1) * PART) for p in range(PARTS)]
    arrivals = [
        [
            pltpu.make_async_copy(source.at[:, part], target.at[:, part], in_sems.at[p, n])
            for n, (source, target) in enumerate(
                ((k_hbm, k_ref), (v_hbm, v_ref), (q_hbm, q_ref), (g_hbm, g_ref))
            )
        ]
        for p, part in enumerate(parts)
    ]
    for group in arrivals:
        for copy in group:
            copy.start()
    departures = []
    for p in range(PARTS):
        for copy in arrivals[p]:
            copy.wait()
        heads = PART // HEAD_SIZE
        for head in range(p * heads, (p + 1) * heads):
            columns = slice(head // 2 * WIDTH, (head // 2 + 1) * WIDTH)
            out_ref[slot_of(head, x_hi)] = lane_pair(
                k_ref[:, columns], v_ref[:, columns], head % 2
            )
            out_ref[slot_of(head, 1 - x_hi)] = lane_pair(
                q_ref[:, columns], g_ref[:, columns], head % 2
            )
        for n in range(2):
            slots = pl.ds(slot_of(p * heads, n), heads)
            copy = pltpu.make_async_copy(out_ref.at[slots], out_hbm.at[slots], out_sems.at[p, n])
            copy.start()
            departures.append(copy)
    for copy in departures:
        copy.wait()


def unpack_kernel(
    in_ref, o_hbm, dq_hbm, dk_hbm, dv_hbm, o_ref, dq_ref, dk_ref, dv_ref, sems
):
    x_hi = lax.axis_index("x_hi")
    copies = []
    for pair in range(HEADS // 2):
        columns = slice(pair * WIDTH, (pair + 1) * WIDTH)
        even, odd = 2 * pair, 2 * pair + 1
        kv0, kv1 = in_ref[slot_of(even, x_hi)], in_ref[slot_of(odd, x_hi)]
        qo0, qo1 = in_ref[slot_of(even, 1 - x_hi)], in_ref[slot_of(odd, 1 - x_hi)]
        dk_ref[:, columns] = turned_pair(kv0, kv1, 0)
        dv_ref[:, columns] = turned_pair(kv0, kv1, 1)
        dq_ref[:, columns] = lane_pair(qo0, qo1, 0)
        o_ref[:, columns] = lane_pair(qo0, qo1, 1)
        if (pair + 1) * WIDTH % PART == 0:
            p = pair * WIDTH // PART
            part = slice(p * PART, (p + 1) * PART)
            for n, (source, target) in enumerate(
                ((o_ref, o_hbm), (dq_ref, dq_hbm), (dk_ref, dk_hbm), (dv_ref, dv_hbm))
            ):
                copy = pltpu.make_async_copy(source.at[:, part], target.at[:, part], sems.at[p, n])
                copy.start()
                copies.append(copy)
    for copy in copies:
        copy.wait()


def split_kernel(in_ref, kv_ref, qg_ref, near_ref, far_ref):
    core = lax.axis_index("core")
    kv_at = core * HALF
    kv_ref[...] = in_ref[pl.ds(kv_at, HALF)]
    qg_ref[...] = in_ref[pl.ds((1 - core) * HALF, HALF)]
    near_ref[...] = in_ref[pl.ds(kv_at + core * QUARTER, QUARTER)]
    far_ref[...] = in_ref[pl.ds(kv_at + (1 - core) * QUARTER, QUARTER)]


def copy_kernel(in_ref, out_ref):
    out_ref[...] = in_ref[...]


def near_kernel(list_hbm, qg_ref, own_ref, mate_ref, near_ref, qo_ref, sums, *scratch):
    sums[...] = jnp.zeros_like(sums)
    core = lax.axis_index("core")
    attend(core, list_hbm, qg_ref, own_ref, mate_ref, (near_ref,), qo_ref, sums, *scratch)


def far_kernel(
    list_hbm, qg_ref, own_ref, mate_ref, near_ref, far_ref, sums_ref,
    qo_ref, own_out, mate_out, halo_out, sums, *scratch,
):
    sums[...] = sums_ref[...]
    core = lax.axis_index("core")
    attend(
        1 - core, list_hbm, qg_ref, own_ref, mate_ref, (near_ref, far_ref), qo_ref, sums, *scratch
    )
    own_at = 2 * core * HALF
    halo_out[...] = sums[pl.ds(2 * HALF - own_at, HALF)].astype(jnp.bfloat16)
    mate_out[...] = sums[HALF : 2 * HALF].astype(jnp.bfloat16)
    own_out[...] = sums[pl.ds(own_at, HALF)]


def attend(
    group, list_hbm, qg_ref, own_ref, mate_ref, halo_refs, qo_ref, accum,
    window, both_even, both_odd, pair_even, pair_odd, listed, table, sem,
):
    core, z = lax.axis_index("core"), lax.axis_index("z")
    own_at = 2 * core * HALF
    halo_at = 2 * HALF - own_at
    first = group * QUARTER
    first_query = z * PLANE + (1 - core) * HALF + first
    first_key = z * PLANE - core * HALF
    lanes = listed.shape[1]
    at = lax.div(first_query, lanes) * lanes
    copy = pltpu.make_async_copy(
        list_hbm.at[:, pl.ds(pl.multiple_of(at, lanes), lanes)], listed, sem
    )
    copy.start()
    window[pl.ds(own_at, HALF)] = own_ref[...]
    window[HALF : 2 * HALF] = mate_ref[...]
    for side, halo_ref in zip((core, 1 - core), halo_refs):
        window[pl.ds(halo_at + side * QUARTER, QUARTER)] = halo_ref[...]
    copy.wait()

    def note(i, carry):
        for s in range(SLOTS):
            block = listed[s, first_query - at + i]
            dead = (block == first_query + i) if s else False
            table[i, s] = jnp.where(dead, -1, block - first_key)
        return carry

    lax.fori_loop(0, QUARTER, note, 0)

    def blocks_of(i):
        return [
            jnp.where(table[i, s] < 0, table[i, 0], table[i, s]) if s else table[i, 0]
            for s in range(SLOTS)
        ]

    left = lax.broadcasted_iota(jnp.int32, (BLOCK, WIDTH), 1) < HEAD_SIZE

    def query_rows(i):
        qg = qg_ref[first + i]
        zero = jnp.zeros_like(qg)
        return jnp.concatenate(
            [jnp.where(left, qg * jnp.bfloat16(SCALING), zero), jnp.where(left, zero, qg)], axis=0
        )

    top = lax.broadcasted_iota(jnp.int32, (WIDTH, BLOCK), 0) < HEAD_SIZE

    def query_columns(i):
        columns = qg_ref[first + i].T
        zero = jnp.zeros_like(columns)
        return jnp.concatenate(
            [jnp.where(top, columns * jnp.bfloat16(SCALING), zero), jnp.where(top, zero, columns)],
            axis=1,
        )

    def products(i, both):
        rows, blocks = query_rows(i), blocks_of(i)
        for k in range(PIECES):
            kv = jnp.concatenate([window[b] for b in blocks[k * PAIR : (k + 1) * PAIR]], axis=0)
            both[:, k * SPAN : (k + 1) * SPAN] = lax.dot_general(
                rows, kv, (((1,), (1,)), ((), ())), preferred_element_type=jnp.float32
            )
            yield

    def weigh(i, both, pair):
        live = [table[i, s] >= 0 for s in range(SLOTS)]
        for r in range(0, BLOCK, CHUNK):
            scores = jnp.concatenate(
                [
                    jnp.where(live[s], both[r : r + CHUNK, s * BLOCK : (s + 1) * BLOCK], -jnp.inf)
                    for s in range(SLOTS)
                ],
                axis=1,
            )
            dprob = both[BLOCK + r : BLOCK + r + CHUNK]
            weights = jnp.exp(scores - jnp.max(scores, axis=1, keepdims=True))
            probs = weights * (1.0 / jnp.sum(weights, axis=1, keepdims=True))
            terms = probs * dprob
            dscore = terms - probs * jnp.sum(terms, axis=1, keepdims=True)
            pair[r : r + CHUNK] = dscore.astype(jnp.bfloat16)
            pair[BLOCK + r : BLOCK + r + CHUNK] = probs.astype(jnp.bfloat16)
            if (r // CHUNK + 1) % (BLOCK // CHUNK // PIECES) == 0:
                yield

    def results(i, pair):
        blocks = blocks_of(i)
        columns = query_columns(i)
        mixed = None
        for k in range(PIECES):
            stacked = pair[:, k * SPAN : (k + 1) * SPAN]
            here = blocks[k * PAIR : (k + 1) * PAIR]
            kv = jnp.concatenate([window[b] for b in here], axis=0)
            part = jnp.dot(stacked, kv, preferred_element_type=jnp.float32)
            mixed = part if mixed is None else mixed + part
            grads = jnp.dot(columns, stacked, preferred_element_type=jnp.float32)
            for s, block in enumerate(here):
                accum[block] += grads[:, s * BLOCK : (s + 1) * BLOCK]
            if k == PIECES - 1:
                qo_ref[i] = jnp.where(left, mixed[:BLOCK] * SCALING, mixed[BLOCK:]).astype(
                    jnp.bfloat16
                )
            yield

    both, pair = (both_even, both_odd), (pair_even, pair_odd)
    for i in range(-1, QUARTER + 1):
        stages = []
        if i + 1 < QUARTER:
            stages.append(products(i + 1, both[(i + 1) % 2]))
        if 0 <= i < QUARTER:
            stages.append(weigh(i, both[i % 2], pair[i % 2]))
        if i > 0:
            stages.append(results(i - 1, pair[(i - 1) % 2]))
        for _ in zip(*stages):
            pass


def halo_sum_kernel(own_ref, halo_ref, out_ref):
    out_ref[...] = own_ref[...] + halo_ref[...].astype(jnp.float32)


def sum_kernel(near_ref, far_ref, own_ref, mate_ref, out_ref):
    core = lax.axis_index("core")
    total = own_ref[...] + mate_ref[...].astype(jnp.float32)
    out_ref[pl.ds(core * HALF, HALF)] = total.astype(jnp.bfloat16)
    query_at = (1 - core) * HALF
    out_ref[pl.ds(query_at + core * QUARTER, QUARTER)] = near_ref[...]
    out_ref[pl.ds(query_at + (1 - core) * QUARTER, QUARTER)] = far_ref[...]


VMEM = pl.BlockSpec(memory_space=pltpu.VMEM)
ANY = pl.BlockSpec(memory_space=pl.ANY)
PARAMS = pltpu.CompilerParams(vmem_limit_bytes=VMEM_LIMIT)
EDGE_PARAMS = pltpu.CompilerParams(vmem_limit_bytes=60 * 1024 * 1024)


def moved(value, axes, target):
    sizes = [lax.axis_size(a) for a in axes]
    pairs = []
    for source in range(int(np.prod(sizes))):
        spot = [int(t) for t in np.unravel_index(source, sizes)]
        goal = target(*spot)
        if all(0 <= g < size for g, size in zip(goal, sizes)):
            pairs.append((source, int(np.ravel_multi_index(goal, sizes))))
    return lax.ppermute(value, axes, pairs)


def to_mate(value):
    return moved(value, ("core",), lambda c: (1 - c,))


def per_device(queries, key_rows, value_rows, cotangent, block_list):
    plane = jax.ShapeDtypeStruct((PLANE, BLOCK, WIDTH), jnp.bfloat16)
    packed = pl.pallas_call(
        pack_kernel,
        out_shape=plane,
        in_specs=[ANY] * 4,
        out_specs=ANY,
        scratch_shapes=[pltpu.VMEM(queries.shape, jnp.bfloat16)] * 4
        + [
            pltpu.VMEM(plane.shape, jnp.bfloat16),
            pltpu.SemaphoreType.DMA((PARTS, 4)),
            pltpu.SemaphoreType.DMA((PARTS, 2)),
        ],
        compiler_params=EDGE_PARAMS,
        name="pack",
    )(queries, key_rows, value_rows, cotangent)
    received = lax.all_to_all(packed, AXES, 0, 0, tiled=True)
    half = (HALF, BLOCK, WIDTH)
    quarter = (QUARTER, BLOCK, WIDTH)
    sums = (3 * HALF, BLOCK, WIDTH)
    key_value, query_grad_rows, near_part, far_part = pl.pallas_call(
        split_kernel,
        out_shape=[jax.ShapeDtypeStruct(half, jnp.bfloat16)] * 2
        + [jax.ShapeDtypeStruct(quarter, jnp.bfloat16)] * 2,
        in_specs=[VMEM],
        out_specs=[VMEM] * 4,
        compiler_params=PARAMS,
        name="split",
    )(received)

    def inward(value):
        return moved(value, ("z", "core"), lambda z, c: (z + (1 if c else -1), c))

    near = pl.pallas_call(
        copy_kernel,
        out_shape=jax.ShapeDtypeStruct(quarter, jnp.bfloat16),
        in_specs=[VMEM],
        out_specs=VMEM,
        compiler_params=PARAMS,
        cost_estimate=pl.CostEstimate(flops=1 << 33, bytes_accessed=1 << 20, transcendentals=0),
        name="near_copy",
    )(inward(near_part))
    mate = to_mate(key_value)
    far = inward(far_part)
    scratch = [
        pltpu.VMEM(sums, jnp.bfloat16),
        pltpu.VMEM((2 * BLOCK, KEYS), jnp.float32),
        pltpu.VMEM((2 * BLOCK, KEYS), jnp.float32),
        pltpu.VMEM((2 * BLOCK, KEYS), jnp.bfloat16),
        pltpu.VMEM((2 * BLOCK, KEYS), jnp.bfloat16),
        pltpu.SMEM((SLOTS, LANES), jnp.int32),
        pltpu.SMEM((QUARTER, SLOTS), jnp.int32),
        pltpu.SemaphoreType.DMA,
    ]
    work = pl.CostEstimate(
        flops=QUARTER * 6 * 2 * BLOCK * KEYS * WIDTH,
        bytes_accessed=1 << 20,
        transcendentals=QUARTER * BLOCK * KEYS,
    )
    query_near, near_sums = pl.pallas_call(
        near_kernel,
        out_shape=[
            jax.ShapeDtypeStruct(quarter, jnp.bfloat16),
            jax.ShapeDtypeStruct(sums, jnp.float32),
        ],
        in_specs=[ANY] + [VMEM] * 4,
        out_specs=[VMEM] * 2,
        scratch_shapes=scratch,
        compiler_params=PARAMS,
        cost_estimate=work,
        name="near",
    )(block_list.T, query_grad_rows, key_value, mate, near)
    query_far, own_part, mate_part, halo_part = pl.pallas_call(
        far_kernel,
        out_shape=[
            jax.ShapeDtypeStruct(quarter, jnp.bfloat16),
            jax.ShapeDtypeStruct(half, jnp.float32),
            jax.ShapeDtypeStruct(half, jnp.bfloat16),
            jax.ShapeDtypeStruct(half, jnp.bfloat16),
        ],
        in_specs=[ANY] + [VMEM] * 6,
        out_specs=[VMEM] * 4,
        scratch_shapes=[pltpu.VMEM(sums, jnp.float32)] + scratch,
        compiler_params=PARAMS,
        cost_estimate=work,
        name="far",
    )(block_list.T, query_grad_rows, key_value, mate, near, far, near_sums)
    mate_sum = to_mate(mate_part)
    halo_sum = moved(halo_part, ("z", "core"), lambda z, c: (z + (-1 if c else 1), c))
    own_sum = pl.pallas_call(
        halo_sum_kernel,
        out_shape=jax.ShapeDtypeStruct(half, jnp.float32),
        in_specs=[VMEM] * 2,
        out_specs=VMEM,
        compiler_params=PARAMS,
        name="halo_total",
    )(own_part, halo_sum)
    outgoing = pl.pallas_call(
        sum_kernel,
        out_shape=plane,
        in_specs=[VMEM] * 4,
        out_specs=VMEM,
        compiler_params=PARAMS,
        name="total",
    )(query_near, query_far, own_sum, mate_sum)
    returned = lax.all_to_all(outgoing, AXES, 0, 0, tiled=True)
    rows = jax.ShapeDtypeStruct(queries.shape, jnp.bfloat16)
    return pl.pallas_call(
        unpack_kernel,
        out_shape=[rows] * 4,
        in_specs=[VMEM],
        out_specs=[ANY] * 4,
        scratch_shapes=[pltpu.VMEM(queries.shape, jnp.bfloat16)] * 4
        + [pltpu.SemaphoreType.DMA((PARTS, 4))],
        compiler_params=PARAMS,
        name="unpack",
    )(returned)


def solution(mesh):
    fine = Mesh(mesh.devices.reshape(2, 4, 16, 2, 2), ("x_lo", "y", "z", "x_hi", "core"))
    rows = P(("z", "x_hi", "core", "x_lo", "y"), None)
    return jax.shard_map(
        per_device,
        mesh=fine,
        in_specs=(rows,) * 4 + (P(),),
        out_specs=(rows,) * 4,
        check_vma=False,
    )
```
